32 devices in a mesh: fsdp: 8 (over z, x), dp: 4 (over y, core).
Axes of the slice: x: 2, y: 2, z: 4, core: 2. Of those that a mesh axis runs over, the one named last changes fastest.
Arguments:
- tokens: bfloat16 [16384, 768], P(('fsdp', 'dp')), may hold values from -6 to 6
- cotangent: bfloat16 [16384, 768], P(('fsdp', 'dp')), may hold values from -6 to 6
- seq_lens: int32 [32, 4], P(('fsdp', 'dp')), may hold values from 0 to 512, as said below
- routes: int32 [16384, 1], P(('fsdp', 'dp')), may hold values from 0 to 7; in each aligned block of 512 rows (0 to 511, 512 to 1023, ...) at most 128 rows name the same one
- norm_gains: bfloat16 [2, 768], P(None, ('fsdp', 'dp')), may hold values from 0.5 to 1.5
- qkv_weight: bfloat16 [768, 2304], P(('fsdp', 'dp')), may hold values from -0.21875 to 0.21875
- out_weight: bfloat16 [768, 768], P(('fsdp', 'dp')), may hold values from -0.875 to 0.875
- router_weight: bfloat16 [768, 8], P(('fsdp', 'dp')), may hold values from -0.15625 to 0.15625
- rel_bias: float32 [32, 12], replicated, may hold values from -4 to 4
- expert_in: bfloat16 [8, 768, 3072], P('dp', None, 'fsdp'), may hold values from -0.21875 to 0.21875
- expert_out: bfloat16 [8, 3072, 768], P('dp', 'fsdp'), may hold values from -0.875 to 0.875
Outputs:
- mixed: bfloat16 [16384, 768], P(('fsdp', 'dp'))
- tokens_grad: float32 [16384, 768], P(('fsdp', 'dp'))
- gains_grad: float32 [2, 768], P(None, ('fsdp', 'dp'))
- qkv_grad: float32 [768, 2304], P(('fsdp', 'dp'))
- out_grad: float32 [768, 768], P(('fsdp', 'dp'))
- router_grad: float32 [768, 8], P(('fsdp', 'dp'))
- bias_grad: float32 [32, 12], replicated
- expert_in_grad: float32 [8, 768, 3072], P('dp', None, 'fsdp')
- expert_out_grad: float32 [8, 3072, 768], P('dp', 'fsdp')
The draws below stay inside these ranges and needn't reach their ends.
Inputs may be any that keep to these rules, and one draw needn't show every extreme that they name: `seq_lens`: row b lists the sequences of block b in order from its first slot; a row sums to 256 or more and to 512 or less; some row is one sequence of 512. `routes`: among the 512 rows of one device no expert is named more than 128 times.
All inputs are finite; a program needn't handle non-finite values.
Results may differ from the reference program's by a relative error of at most 0.015.
Values may be sent and summed in bfloat16 or wider, within the bound.
No kernel may reach another device: no remote copies, remote signals or barrier semaphores. Data moves between devices by JAX's collectives and lax.ppermute only.
A program may use at most 192 MiB of HBM per device.

```python
import math
from functools import reduce
import jax
import jax.numpy as jnp
import numpy as np
from jax import lax

D = 768
HEADS = 12
HEAD_DIM = 64
FF = 3072
BUCKETS = 32
TOK_DEV = 512
SEQS_DEV = 4
EXPERTS = 8
CAP = 128
TOKENS = 16384
DEVICES = 32


def draw_seq_lens(key, part):
    key = jax.random.fold_in(key, 11)
    key_total, key_cut, key_full = jax.random.split(key, 3)
    totals = jax.random.randint(key_total, (DEVICES, 1), TOK_DEV // 2, TOK_DEV + 1, dtype=jnp.int32)
    full_row = jax.random.randint(key_full, (), 0, DEVICES, dtype=jnp.int32)
    row_ids = jnp.arange(DEVICES, dtype=jnp.int32)[:, None]
    totals = jnp.where(row_ids == full_row, TOK_DEV, totals)
    cuts = jax.random.randint(key_cut, (DEVICES, SEQS_DEV - 1), 0, totals + 1, dtype=jnp.int32)
    cuts = jnp.sort(cuts, axis=1)
    edges = jnp.concatenate([jnp.zeros((DEVICES, 1), jnp.int32), cuts, totals], axis=1)
    lengths = edges[:, 1:] - edges[:, :-1]
    single = jnp.zeros_like(lengths).at[:, 0].set(TOK_DEV)
    return jnp.where(row_ids == full_row, single, lengths).astype(jnp.int32)


def levels(stream_key, extent, shards, smallest, high):
    def one(axis_at, shards_of):
        heights = jax.random.uniform(jax.random.fold_in(jax.random.fold_in(stream_key, 6), axis_at), (shards_of,), jnp.float32, smallest / len(shards), high / len(shards))
        return jnp.repeat(jnp.exp(heights), extent[axis_at] // shards_of).reshape((-1,) + (1,) * (len(extent) - axis_at - 1))

    loudness = one(*shards[0])
    for cut in shards[1:]:
        loudness = loudness * one(*cut)
    return loudness


def shared_out(key, own, number, rows, amount, top, most, lean):
    sequence = jax.random.permutation(key, amount)
    heavy_load, ordinary = shares(amount, rows * top, most, lean, True), shares(amount, rows * top, most, lean, False)
    places = jnp.arange(amount)

    def named(sizes, turn):
        used = int((sizes > 0).sum())
        fixed = max(1, used // 4)
        moved = fixed + (places - fixed + turn * (used - fixed)) % max(1, amount - fixed)
        return jnp.zeros((amount,), jnp.int32).at[sequence[jnp.where(places < fixed, places, moved)]].set(jnp.asarray(sizes, jnp.int32))

    sizes = jnp.where(number % 4 == 0, named(heavy_load, number // 4), named(ordinary, number - number // 4 - 1))
    mixed = jax.random.permutation(jax.random.fold_in(own, 3), amount)
    source_of, taker = mixed[0:amount // 2 * 2:2], mixed[1:amount // 2 * 2:2]
    room = jnp.minimum(sizes[source_of] - 1, most - sizes[taker]) // 2
    room = jnp.where((source_of == sequence[0]) | (taker == sequence[0]) | (sizes[taker] == 0), 0, jnp.maximum(room, 0))
    moved = jax.random.randint(jax.random.fold_in(own, 4), (amount // 2,), 0, 1 << 20) % (room + 1)
    sizes = sizes.at[source_of].add(-moved).at[taker].add(moved)
    items = jnp.searchsorted(jnp.cumsum(sizes), jnp.arange(rows * top), side="right").astype(jnp.int32)
    listing = items.reshape(top, rows).T
    listing = listing[jax.random.permutation(jax.random.fold_in(own, 1), rows)]
    turn = jax.random.randint(jax.random.fold_in(own, 2), (rows, 1), 0, top)
    return jnp.take_along_axis(listing, (jnp.arange(top)[None, :] + turn) % top, axis=1)


def shares(amount, total, reach, skew, full):
    loads = [(1 << 20) // math.isqrt(rank ** skew) + 1 for rank in range(1, amount + 1)]
    largest = reach if full else min(reach, max(-(-total // amount), total * loads[0] // sum(loads)))
    least = 1 if total - largest >= amount - 1 else 0
    holding, rest = [largest] + [least] * (amount - 1), total - largest - least * (amount - 1)
    while rest > 0:
        free = [i for i in range(1, amount) if holding[i] < largest] or [i for i in range(1, amount) if holding[i] < reach]
        pool, remaining = sum([loads[i] for i in free]), rest
        for i in free:
            addition = min(reach - holding[i], max(1, remaining * loads[i] // pool), rest)
            holding[i] = holding[i] + addition
            rest = rest - addition
    return np.array(holding)


def centred(own_key, extent, deviation, limit, pieces=(), kind=jnp.bfloat16):
    array = jax.random.normal(own_key, extent, jnp.float32) * deviation
    if len(pieces) > 0:
        array = levels(own_key, extent, pieces, -0.22, 0.18) * array
    return jnp.clip(array, min=-limit, max=limit).astype(kind)


def setup_inputs(seed: int = 0) -> dict:
    splits = jax.random.split(jax.random.key(seed), 12)
    tokens = centred(splits[0], (TOKENS, D), 1.0, 6.0, ((0, 32),))
    cotangent = centred(splits[1], (TOKENS, D), 1.0, 6.0, ((0, 32),))
    seq_lens = draw_seq_lens(jax.random.fold_in(splits[11], 71), 0)
    routes_keys = jax.random.split(jax.random.fold_in(splits[3], 1), TOKENS // TOK_DEV)
    routes_turns = jax.random.permutation(jax.random.fold_in(splits[3], 3), TOKENS // TOK_DEV)
    routes = jax.vmap(lambda own, number: shared_out(jax.random.fold_in(splits[3], 2), own, number, TOK_DEV, EXPERTS, 1, CAP, 2))(routes_keys, routes_turns).reshape((TOKENS, 1))
    norm_gains = jnp.clip(1.0 + 0.1 * jax.random.normal(splits[4], (2, D), jnp.float32), 0.5, 1.5).astype(jnp.bfloat16)
    qkv_weight = centred(splits[5], (D, 3 * D), D ** -0.5, 0.21875, ((0, 32),))
    out_weight = centred(splits[6], (D, D), (D // 16) ** -0.5, 0.875, ((0, 32),))
    router_weight = centred(splits[7], (D, EXPERTS), (2 * D) ** -0.5, 0.15625, ((0, 32),))
    rel_bias = centred(splits[8], (BUCKETS, HEADS), 1.0, 4.0, (), jnp.float32)
    expert_in = centred(splits[9], (EXPERTS, D, FF), D ** -0.5, 0.21875, ((0, 4), (2, 8)))
    expert_out = centred(splits[10], (EXPERTS, FF, D), (max(FF // (EXPERTS * EXPERTS), 1)) ** -0.5, 0.875, ((0, 4), (1, 8)))
    return dict(tokens=tokens, cotangent=cotangent, seq_lens=seq_lens, routes=routes, norm_gains=norm_gains, qkv_weight=qkv_weight, out_weight=out_weight, router_weight=router_weight, rel_bias=rel_bias, expert_in=expert_in, expert_out=expert_out)


EPS = 1e-06
LIMITS = (12, 16, 23, 32, 46, 64, 91)
SCALE = 0.125
HIGH = lax.Precision.HIGHEST

@jax.custom_vjp
def low(v):
    return lax.optimization_barrier(v.astype(jnp.bfloat16)).astype(jnp.float32)

@jax.custom_vjp
def low_back(v):
    return v

def low_keep(v):
    return (low(v), None)

def low_pass(kept, grad):
    return (grad,)

def back_keep(v):
    return (v, None)

def back_low(kept, grad):
    return (low(grad),)
low.defvjp(low_keep, low_pass)
low_back.defvjp(back_keep, back_low)

def both_ways(values):
    return low(low_back(values))

def bucket_index(relative):
    distance = jnp.abs(relative)
    far_bucket = reduce(lambda counted, boundary: counted + (distance >= boundary).astype(jnp.int32), LIMITS, jnp.full_like(distance, 8))
    return jnp.where(distance < 8, distance, far_bucket) + 16 * (relative > 0).astype(jnp.int32)

def segment_ids(lengths, slots):
    ending = jnp.cumsum(lengths).astype(jnp.int32)
    places = jnp.arange(slots, dtype=jnp.int32)
    return lax.optimization_barrier(jnp.sum((places[:, None] >= ending[None, :]).astype(jnp.int32), axis=1))

def rms_norm(values, gain):
    return values * lax.rsqrt(lax.optimization_barrier(jnp.mean(values * values, axis=-1, keepdims=True)) + EPS) * gain

def softmax_rows(scores):
    highest = lax.optimization_barrier(jnp.max(scores, axis=-1, keepdims=True))
    raised = jnp.exp(scores - highest)
    return raised / lax.optimization_barrier(jnp.sum(raised, axis=-1, keepdims=True))

def attend_device(parts, bias_heads):
    queries, keys_in, values_in, lengths = parts
    segment = segment_ids(lengths, queries.shape[0])
    allowed = segment[:, None] == segment[None, :]
    scores = jnp.einsum('qhd,khd->hqk', queries, keys_in, precision=HIGH) * SCALE + bias_heads
    scores = low_back(scores)
    soft = low(softmax_rows(jnp.where(allowed[None], scores, -1e+30)))
    return jnp.einsum('hqk,khd->qhd', soft, values_in, precision=HIGH)

def destinations(chosen):
    per_device = chosen.reshape(DEVICES, TOK_DEV)
    hot_table = (per_device[:, :, None] == jnp.arange(EXPERTS, dtype=jnp.int32)[None, None, :]).astype(jnp.int32)
    earlier = (jnp.cumsum(hot_table, axis=1) - hot_table).astype(jnp.int32)
    rank_in = lax.optimization_barrier(jnp.sum(earlier * hot_table, axis=2)).astype(jnp.int32)
    device_ids = jnp.arange(DEVICES, dtype=jnp.int32)[:, None]
    return (per_device * (DEVICES * CAP) + device_ids * CAP + rank_in).reshape(-1).astype(jnp.int32)

def run_expert(parts):
    expert_rows, w_first, w_second = parts
    pre_act = low_back(jnp.dot(expert_rows, w_first, precision=HIGH))
    hidden = low(jax.nn.gelu(pre_act, approximate=False))
    return both_ways(jnp.dot(hidden, w_second, precision=HIGH))

def forward(inputs, qkv_w, out_w, gains, table, router_w, w_first, w_second, seq_lens, routes, buckets):
    slots = inputs.shape[0]
    xn_one = low(rms_norm(inputs, gains[0]))
    projected = both_ways(jnp.dot(xn_one, qkv_w, precision=HIGH))
    head_shape = (DEVICES, TOK_DEV, HEADS, HEAD_DIM)
    queries = projected[:, :D].reshape(head_shape)
    keys_in = projected[:, D:2 * D].reshape(head_shape)
    values_in = projected[:, 2 * D:].reshape(head_shape)
    bias_heads = jnp.moveaxis(table[buckets], 2, 0)

    def one_device(parts):
        return attend_device(parts, bias_heads)
    attended = lax.map(jax.checkpoint(one_device), (queries, keys_in, values_in, seq_lens))
    attended = both_ways(attended.reshape(slots, D))
    hidden_one = inputs + low_back(jnp.dot(attended, out_w, precision=HIGH))
    xn_two = low(rms_norm(hidden_one, gains[1]))
    router_soft = softmax_rows(jnp.dot(xn_two, router_w, precision=HIGH))
    chosen = routes[:, 0]
    chosen_hot = chosen[:, None] == jnp.arange(EXPERTS, dtype=jnp.int32)[None, :]
    gate_value = lax.optimization_barrier(jnp.sum(jnp.where(chosen_hot, router_soft, 0.0), axis=1))
    target = destinations(chosen)
    buffer = jnp.zeros((EXPERTS * DEVICES * CAP, D), inputs.dtype).at[target].set(low_back(xn_two))
    buffer = buffer.reshape(EXPERTS, DEVICES * CAP, D)
    expert_y = lax.map(jax.checkpoint(run_expert), (buffer, w_first, w_second))
    token_y = expert_y.reshape(EXPERTS * DEVICES * CAP, D)[target]
    return hidden_one + gate_value[:, None] * token_y

def reference(tokens, cotangent, seq_lens, routes, norm_gains, qkv_weight, out_weight, router_weight, rel_bias, expert_in, expert_out):
    places = jnp.arange(TOK_DEV, dtype=jnp.int32)
    buckets = bucket_index(places[None, :] - places[:, None])

    def layer(inputs, gains, qkv_w, out_w, router_w, table, w_first, w_second):
        return forward(inputs, qkv_w, out_w, gains, table, router_w, w_first, w_second, seq_lens, routes, buckets)
    floats = tuple((item.astype(jnp.float32) for item in (tokens, norm_gains, qkv_weight, out_weight, router_weight, rel_bias, expert_in, expert_out)))
    mixed, pull = jax.vjp(layer, *floats)
    grads = pull(cotangent.astype(jnp.float32))
    return (mixed.astype(jnp.bfloat16), grads[0], grads[1], grads[2], grads[3], grads[4], grads[5], grads[6], grads[7])
```

```python
from functools import partial, reduce

import jax
import jax.numpy as jnp
from jax import lax
from jax.experimental import pallas as pl
from jax.experimental.pallas import tpu as pltpu
from jax.sharding import PartitionSpec as P

HEADS = 12
HEAD_DIM = 64
EPS = 1e-06
LIMITS = (12, 16, 23, 32, 46, 64, 91)
SCALE = 0.125
HIGH = lax.Precision.HIGHEST
LOW = jnp.bfloat16
FULL = jnp.float32
ROWS = 128
VMEM_BYTES = 52 * 1024 * 1024


def bucket_index(relative):
    distance = jnp.abs(relative)
    far_bucket = reduce(
        lambda counted, boundary: counted + (distance >= boundary).astype(jnp.int32),
        LIMITS,
        jnp.full_like(distance, 8),
    )
    return jnp.where(distance < 8, distance, far_bucket) + 16 * (relative > 0).astype(jnp.int32)


def segment_ids(lengths, slots):
    ending = jnp.cumsum(lengths)
    places = jnp.arange(slots, dtype=jnp.int32)
    return jnp.sum((places[:, None] >= ending[None, :]).astype(jnp.int32), axis=1)


def rms_parts(values, gain):
    inverse = lax.rsqrt(jnp.mean(values * values, axis=-1, keepdims=True) + EPS)
    return (values * inverse * gain, inverse)


def norm_back(values, inverse, gain, upstream):
    scaled = upstream * gain
    grad_values = inverse * scaled - values * inverse * inverse * inverse * jnp.mean(
        values * scaled, axis=-1, keepdims=True
    )
    return (grad_values, jnp.sum(upstream * values * inverse, axis=0))


def softmax_rows(scores):
    highest = jnp.max(scores, axis=-1, keepdims=True)
    raised = jnp.exp(scores - highest)
    return raised / jnp.sum(raised, axis=-1, keepdims=True)


def mm(left, right, contract, out=FULL):
    return lax.dot_general(left, right, (contract, ((), ())), preferred_element_type=FULL).astype(
        out
    )


def swap(value, dim):
    axis, mask = dim
    count = lax.axis_size(axis)
    return lax.ppermute(value, axis, [(i, i ^ mask) for i in range(count)])


def bit_of(dim):
    axis, mask = dim
    return (lax.axis_index(axis) & mask) != 0


def stage_pair(value, dim):
    other = swap(value, dim)
    return jnp.where(bit_of(dim), jnp.stack((other, value)), jnp.stack((value, other)))


def line_shift(value, places, first, last, by):
    pairs = []
    for place in range(first, last + 1):
        if 0 <= place + by < places:
            pairs += [(2 * place, 2 * (place + by)), (2 * place + 1, 2 * (place + by) + 1)]
    return lax.ppermute(value, "fsdp", pairs)


def ring_shift(value, places, by):
    count = 2 * places
    return lax.ppermute(value, "fsdp", [(i, (i - 2 * by) % count) for i in range(count)])


def z_gather(value, places, place):
    parts = jnp.stack([value] + [ring_shift(value, places, by) for by in range(1, places)])
    return lax.dynamic_slice_in_dim(
        jnp.concatenate((parts, parts)), lax.rem(places - place, places), places, 0
    )


def line_gather(value, places, place):
    ahead, behind = [value], [value]
    for step in range(1, places):
        ahead.append(line_shift(ahead[-1], places, 1, places - step, -1))
        behind.append(line_shift(behind[-1], places, step - 1, places - 2, 1))
    return [value] + [
        jnp.where(place + step < places, ahead[step], behind[places - step])
        for step in range(1, places)
    ]


def line_scatter(parts, places):
    up = down = None
    for far in range(places - 1, 0, -1):
        send_up, send_down = parts[far], parts[places - far]
        if up is not None:
            send_up = (send_up.astype(FULL) + up.astype(FULL)).astype(LOW)
            send_down = (send_down.astype(FULL) + down.astype(FULL)).astype(LOW)
        up = line_shift(send_up, places, 0, places - 1 - far, 1)
        down = line_shift(send_down, places, far, places - 1, -1)
    return parts[0].astype(FULL) + up.astype(FULL) + down.astype(FULL)


def gather_blocks(value, dims):
    held = {(): value}
    for dim in dims:
        keys = list(held)
        arrived = swap(jnp.stack([held[key] for key in keys]) if len(keys) > 1 else value, dim)
        for number, key in enumerate(keys):
            new_key = tuple(sorted(key + (dim,)))
            held[new_key] = arrived[number] if len(keys) > 1 else arrived
    return held


def scatter_blocks(held, dims):
    for dim in dims:
        stay = [key for key in held if dim not in key]
        leave = [tuple(sorted(key + (dim,))) for key in stay]
        sent = jnp.stack([held[key].astype(LOW) for key in leave])
        arrived = swap(sent, dim)
        held = {
            key: held[key].astype(FULL) + arrived[number].astype(FULL)
            for number, key in enumerate(stay)
        }
    return held[()]


def dense_gather(value, places, place, dims, core):
    rows, columns = value.shape
    half = (columns // 256) * 128
    first = z_gather(value[:, :half], places, place)
    for dim in dims:
        first = stage_pair(first, dim)
    second = value[:, half:]
    for dim in reversed(dims):
        second = stage_pair(second, dim)
    second = z_gather(second, places, place)
    first, second = (stage_pair(part, core) for part in (first, second))
    count = len(dims)
    axes = ("core",) + tuple(reversed(dims)) + ("z", "rows", "columns")
    axes_second = ("core", "z") + tuple(dims) + ("rows", "columns")
    wanted = ("z", dims[0]) + tuple(sorted(dims[1:], reverse=True)) + ("core", "rows", "columns")
    assert count + 4 == len(wanted)
    first = first.transpose([axes.index(name) for name in wanted]).reshape(-1, half)
    second = second.transpose([axes_second.index(name) for name in wanted]).reshape(
        -1, columns - half
    )
    return jnp.concatenate((first, second), axis=1)


def dense_scatter(value, places, place, dims, core, rows):
    columns = value.shape[1]
    half = (columns // 256) * 128
    names = ["z", dims[0]] + sorted(dims[1:], reverse=True) + [core]
    shaped = value.reshape((places,) + (2,) * (len(names) - 1) + (rows, columns))

    def halve(part, part_names, dim):
        spot = part_names.index(dim)
        own = bit_of(dim).astype(jnp.int32)
        keep = lax.dynamic_index_in_dim(part, own, spot, keepdims=False)
        send = lax.dynamic_index_in_dim(part, 1 - own, spot, keepdims=False)
        total = keep.astype(FULL) + swap(send, dim).astype(FULL)
        return (total, part_names[:spot] + part_names[spot + 1 :])

    def run(part, order):
        part_names = names
        for dim in order:
            total, part_names = halve(part, part_names, dim)
            part = total.astype(LOW)
        total = total if places == 1 else lax.dynamic_index_in_dim(total, place, 0, keepdims=False)
        for by in range(1, places):
            send = lax.dynamic_index_in_dim(part, lax.rem(place + by, places), 0, keepdims=False)
            total = total + ring_shift(send, places, places - by).astype(FULL)
        return total

    first = run(shaped[..., :half], [core] + list(dims))
    second = run(shaped[..., half:], [core] + list(reversed(dims)))
    return jnp.concatenate((first, second), axis=1)


def sum_everywhere(value):
    for axis in ("dp", "fsdp"):
        mask = 1
        while mask < lax.axis_size(axis):
            value = value + swap(value, (axis, mask))
            mask *= 2
    return value


def diagonal_hot(slots, bucket_count):
    width = 2 * slots
    lanes = jnp.arange(width, dtype=jnp.int32)[None, :]
    rows = jnp.arange(8, dtype=jnp.int32)[:, None]
    diagonal = (lanes - rows + (ROWS - 1)) % width
    bucket = jnp.where(diagonal < width - 1, bucket_index(diagonal - (slots - 1)), -1)
    return (bucket[:, :, None] == jnp.arange(bucket_count, dtype=jnp.int32)).astype(FULL)


def attend_kernel(query, key, value, base, seg_col, seg_row, out, probs, toeplitz):
    slots = query.shape[0]
    lanes = lax.broadcasted_iota(jnp.int32, (1, 2 * HEAD_DIM), 1)
    total = [None] * (slots // ROWS)
    for head in range(2):
        mine = (lanes >= head * HEAD_DIM) & (lanes < (head + 1) * HEAD_DIM)
        table = base[head]
        size = 8
        while size < ROWS:
            table = jnp.concatenate((table, pltpu.roll(table, size, 1)), axis=0)
            size *= 2
        toeplitz[...] = table
        value_head = jnp.where(mine, value[...], 0).astype(LOW)
        for block in range(slots // ROWS):
            rows = pl.ds(block * ROWS, ROWS)
            query_head = jnp.where(mine, query[rows, :], 0).astype(LOW)
            shift = slots - ROWS - block * ROWS
            scores = mm(query_head, key[...], ((1,), (1,))) * SCALE
            scores = scores + toeplitz[:, shift : shift + slots]
            scores = jnp.where(seg_col[rows, :] == seg_row[...], scores, -1e30)
            highest = jnp.max(scores, axis=-1, keepdims=True)
            raised = jnp.exp(scores - highest)
            low = (raised / jnp.sum(raised, axis=-1, keepdims=True)).astype(LOW)
            probs[head, rows, :] = low
            part = mm(low, value_head, ((1,), (0,)))
            total[block] = part if head == 0 else total[block] + part
    for block in range(slots // ROWS):
        out[pl.ds(block * ROWS, ROWS), :] = total[block].astype(LOW)


def attend_forward(projected, base, seg_col, seg_row):
    slots = projected.shape[0]
    width = projected.shape[1] // 3
    pairs = HEADS // 2
    lanes = 2 * HEAD_DIM
    return pl.pallas_call(
        attend_kernel,
        grid=(pairs,),
        in_specs=[
            pl.BlockSpec((slots, lanes), lambda p: (0, p)),
            pl.BlockSpec((slots, lanes), lambda p: (0, p + pairs)),
            pl.BlockSpec((slots, lanes), lambda p: (0, p + 2 * pairs)),
            pl.BlockSpec((2, 8, 2 * slots), lambda p: (p, 0, 0)),
            pl.BlockSpec((slots, 1), lambda p: (0, 0)),
            pl.BlockSpec((1, slots), lambda p: (0, 0)),
        ],
        out_specs=[
            pl.BlockSpec((slots, lanes), lambda p: (0, p)),
            pl.BlockSpec((2, slots, slots), lambda p: (p, 0, 0)),
        ],
        out_shape=[
            jax.ShapeDtypeStruct((slots, width), LOW),
            jax.ShapeDtypeStruct((HEADS, slots, slots), LOW),
        ],
        scratch_shapes=[pltpu.VMEM((ROWS, 2 * slots), FULL)],
        compiler_params=pltpu.CompilerParams(vmem_limit_bytes=VMEM_BYTES),
        cost_estimate=pl.CostEstimate(
            flops=HEADS * slots * slots * HEAD_DIM * 16,
            bytes_accessed=HEADS * slots * slots * 2 + 8 * slots * width,
            transcendentals=HEADS * slots * slots,
        ),
        name="attend_forward",
    )(projected, projected, projected, base, seg_col, seg_row)


def attend_back_kernel(
    query, key, value, grad, probs, out_query, out_key, out_value, diagonals, lined, scores_low
):
    slots = query.shape[0]
    lanes = lax.broadcasted_iota(jnp.int32, (1, 2 * HEAD_DIM), 1)
    query_total = [None] * (slots // ROWS)
    key_total = value_total = None
    for head in range(2):
        mine = (lanes >= head * HEAD_DIM) & (lanes < (head + 1) * HEAD_DIM)
        key_head = jnp.where(mine, key[...], 0).astype(LOW)
        grad_head = jnp.where(mine, grad[...], 0).astype(LOW)
        query_head = jnp.where(mine, query[...], 0).astype(LOW)
        lined[...] = jnp.zeros_like(lined)
        for block in range(slots // ROWS):
            rows = pl.ds(block * ROWS, ROWS)
            soft = probs[head, rows, :].astype(FULL)
            grad_rows = jnp.where(mine, grad[rows, :], 0).astype(LOW)
            weighted = soft * mm(grad_rows, value[...], ((1,), (1,)))
            back = weighted - soft * jnp.sum(weighted, axis=-1, keepdims=True)
            low = back.astype(LOW)
            scores_low[rows, :] = low
            shift = slots - ROWS - block * ROWS
            lined[:, shift : shift + slots] += low.astype(FULL)
            part = mm(low, key_head, ((1,), (0,)))
            query_total[block] = part if head == 0 else query_total[block] + part
        key_part = mm(scores_low[...], query_head, ((0,), (0,)))
        value_part = mm(probs[head], grad_head, ((0,), (0,)))
        key_total = key_part if head == 0 else key_total + key_part
        value_total = value_part if head == 0 else value_total + value_part
        table = lined[...]
        size = ROWS
        while size > 8:
            size //= 2
            table = table[:size] + pltpu.roll(table[size:], 2 * slots - size, 1)
        diagonals[head] = table
    out_key[...] = (key_total * SCALE).astype(LOW)
    out_value[...] = value_total.astype(LOW)
    for block in range(slots // ROWS):
        out_query[pl.ds(block * ROWS, ROWS), :] = (query_total[block] * SCALE).astype(LOW)


def attend_back(projected, grad_attended, probs):
    slots = projected.shape[0]
    width = projected.shape[1] // 3
    pairs = HEADS // 2
    lanes = 2 * HEAD_DIM
    column = pl.BlockSpec((slots, lanes), lambda p: (0, p))
    return pl.pallas_call(
        attend_back_kernel,
        grid=(pairs,),
        in_specs=[
            column,
            pl.BlockSpec((slots, lanes), lambda p: (0, p + pairs)),
            pl.BlockSpec((slots, lanes), lambda p: (0, p + 2 * pairs)),
            column,
            pl.BlockSpec((2, slots, slots), lambda p: (p, 0, 0)),
        ],
        out_specs=[
            column,
            column,
            column,
            pl.BlockSpec((2, 8, 2 * slots), lambda p: (p, 0, 0)),
        ],
        out_shape=[jax.ShapeDtypeStruct((slots, width), LOW)] * 3
        + [jax.ShapeDtypeStruct((HEADS, 8, 2 * slots), FULL)],
        scratch_shapes=[pltpu.VMEM((ROWS, 2 * slots), FULL), pltpu.VMEM((slots, slots), LOW)],
        compiler_params=pltpu.CompilerParams(vmem_limit_bytes=VMEM_BYTES),
        cost_estimate=pl.CostEstimate(
            flops=HEADS * slots * slots * HEAD_DIM * 32,
            bytes_accessed=HEADS * slots * slots * 2 + 14 * slots * width,
            transcendentals=0,
        ),
        name="attend_back",
    )(projected, projected, projected, grad_attended, probs)


def expert_kernel(chunks, started, *refs):
    refs = list(refs)
    rows, grads = refs[0], refs[1]
    first = refs[2 : 2 + chunks]
    second = refs[2 + chunks : 2 + 2 * chunks]
    at = 2 + 2 * chunks
    if started:
        old_y, old_back = refs[at], refs[at + 1]
        at += 2
    y_out, back_out = refs[at], refs[at + 1]
    first_out = refs[at + 2 : at + 2 + chunks]
    second_out = refs[at + 2 + chunks : at + 2 + 2 * chunks]
    y_sum, back_sum, hidden_low, pre_low = refs[at + 2 + 2 * chunks :]
    count = rows.shape[1]
    step = min(256, count)
    for chunk in range(chunks):
        w_first, w_second = first[chunk], second[chunk]
        for block in range(count // step):
            some = pl.ds(block * step, step)
            pre = mm(rows[0, some, :], w_first[0], ((1,), (0,)))
            grad_hidden = mm(grads[0, some, :], w_second[0], ((1,), (1,)))
            normal_cdf = 0.5 + 0.5 * lax.erf(pre * 0.7071067811865476)
            slope = normal_cdf + pre * jnp.exp(-0.5 * pre * pre) * 0.3989422804014327
            hidden = (pre * normal_cdf).astype(LOW)
            grad_pre = (grad_hidden * slope).astype(LOW)
            hidden_low[some, :] = hidden
            pre_low[some, :] = grad_pre
            y_part = mm(hidden, w_second[0], ((1,), (0,)))
            back_part = mm(grad_pre, w_first[0], ((1,), (1,)))
            if chunk > 0:
                y_part = y_part + y_sum[some, :]
                back_part = back_part + back_sum[some, :]
            elif started:
                y_part = y_part + old_y[0, some, :].astype(FULL)
                back_part = back_part + old_back[0, some, :].astype(FULL)
            if chunk < chunks - 1:
                y_sum[some, :] = y_part
                back_sum[some, :] = back_part
            else:
                y_out[0, some, :] = y_part.astype(LOW)
                back_out[0, some, :] = back_part.astype(LOW)
        first_out[chunk][0] = mm(rows[0], pre_low[...], ((0,), (0,)), LOW)
        second_out[chunk][0] = mm(hidden_low[...], grads[0], ((0,), (0,)), LOW)


def run_experts(rows, grads, first, second, old=()):
    chunks = len(first)
    experts, count, width = rows.shape
    units = first[0].shape[2]

    def whole(*shape):
        return pl.BlockSpec((1,) + shape, lambda e: (e, 0, 0))

    row_spec, first_spec, second_spec = whole(count, width), whole(width, units), whole(units, width)
    outs = pl.pallas_call(
        partial(expert_kernel, chunks, len(old) > 0),
        grid=(experts,),
        in_specs=[row_spec] * 2
        + [first_spec] * chunks
        + [second_spec] * chunks
        + [row_spec] * len(old),
        out_specs=[row_spec] * 2 + [first_spec] * chunks + [second_spec] * chunks,
        out_shape=[jax.ShapeDtypeStruct(rows.shape, LOW)] * 2
        + [jax.ShapeDtypeStruct((experts, width, units), LOW)] * chunks
        + [jax.ShapeDtypeStruct((experts, units, width), LOW)] * chunks,
        scratch_shapes=[
            pltpu.VMEM((count, width), FULL),
            pltpu.VMEM((count, width), FULL),
            pltpu.VMEM((count, units), LOW),
            pltpu.VMEM((count, units), LOW),
        ],
        compiler_params=pltpu.CompilerParams(vmem_limit_bytes=VMEM_BYTES),
        cost_estimate=pl.CostEstimate(
            flops=experts * chunks * 12 * count * width * units,
            bytes_accessed=experts * (8 * count * width + 8 * chunks * width * units),
            transcendentals=2 * experts * chunks * count * units,
        ),
        name="expert_pass",
    )(rows, grads, *first, *second, *old)
    return (outs[0], outs[1], outs[2 : 2 + chunks], outs[2 + chunks :])


def body(
    tokens,
    cotangent,
    seq_lens,
    routes,
    norm_gains,
    qkv_weight,
    out_weight,
    router_weight,
    rel_bias,
    expert_in,
    expert_out,
):
    tok_count, width = tokens.shape
    bucket_count = rel_bias.shape[0]
    shard_rows = qkv_weight.shape[0]
    experts_all = router_weight.shape[1]
    local_experts = expert_in.shape[0]
    capacity = 2 * tok_count // experts_all
    places = lax.axis_size("fsdp") // 2
    place = lax.axis_index("fsdp") // 2
    peer = lax.axis_index("dp")
    peer_count = lax.axis_size("dp")
    core = ("dp", 1)
    dims = [("fsdp", 1)]
    mask = 2
    while mask < peer_count:
        dims.append(("dp", mask))
        mask *= 2

    spare = -(4 * width + experts_all + 2) % 128
    packed = jnp.concatenate(
        (
            qkv_weight,
            out_weight,
            router_weight,
            norm_gains.T,
            jnp.zeros((shard_rows, spare), LOW),
        ),
        axis=1,
    )
    dense = dense_gather(packed, places, place, dims, core)
    qkv_full = dense[:, : 3 * width]
    out_full = dense[:, 3 * width : 4 * width]
    router_full = dense[:, 4 * width : 4 * width + experts_all]
    gains_float = dense[:, 4 * width + experts_all : 4 * width + experts_all + 2].T.astype(FULL)

    first_all = line_gather(expert_in, places, place)
    second_all = line_gather(expert_out, places, place)

    chosen = routes[:, 0]
    chosen_hot = chosen[:, None] == jnp.arange(experts_all, dtype=jnp.int32)[None, :]
    order = jnp.arange(tok_count, dtype=jnp.int32)
    earlier = (order[:, None] > order[None, :]).astype(LOW)
    rank_all = jnp.dot(earlier, chosen_hot.astype(LOW), preferred_element_type=FULL)
    rank_in = jnp.sum(jnp.where(chosen_hot, rank_all, 0.0), axis=1).astype(jnp.int32)
    slots_of = gather_blocks((chosen * capacity + rank_in)[None, :], dims)
    keys = sorted(slots_of)
    slots_near = jnp.stack([slots_of[key][0] for key in keys])
    local_slots = local_experts * capacity
    slot_ids = jnp.arange(local_slots, dtype=jnp.int32).reshape(local_experts, capacity)

    def hot_of(owner):
        wanted = owner * local_slots + slot_ids
        return (slots_near[:, None, None, :] == wanted[None, :, :, None]).astype(LOW)

    hot_own, hot_other = hot_of(peer), hot_of(peer ^ 1)
    segment = segment_ids(seq_lens[0], tok_count)
    bucket_hot = diagonal_hot(tok_count, bucket_count)
    base = jnp.einsum("rjb,bh->hrj", bucket_hot, rel_bias, precision=HIGH)

    inputs = tokens.astype(FULL)
    normed_one, inverse_one = rms_parts(inputs, gains_float[0])
    normed_low = normed_one.astype(LOW)
    projected = jnp.dot(normed_low, qkv_full, preferred_element_type=FULL).astype(LOW)
    attended, probs = attend_forward(projected, base, segment[:, None], segment[None, :])
    hidden_one = inputs + jnp.dot(attended, out_full, preferred_element_type=FULL)
    normed_two, inverse_two = rms_parts(hidden_one, gains_float[1])
    normed_two_low = normed_two.astype(LOW)
    router_soft = softmax_rows(jnp.dot(normed_two_low, router_full, preferred_element_type=FULL))
    gate_value = jnp.sum(jnp.where(chosen_hot, router_soft, 0.0), axis=1)
    upstream = cotangent.astype(FULL)
    grad_y = (gate_value[:, None] * upstream).astype(LOW)

    def dispatch(value, dims_in_order):
        held = gather_blocks(value, dims_in_order)
        blocks = jnp.stack([held[key] for key in keys])

        def pick(hot):
            return jnp.einsum("bjst,btd->jbsd", hot, blocks, preferred_element_type=FULL).astype(LOW)

        both = jnp.stack((pick(hot_own), swap(pick(hot_other), core)), axis=1)
        return both.reshape(local_experts, -1, width)

    rows = dispatch(normed_two_low, dims)
    grads = dispatch(grad_y, list(reversed(dims)))

    odd = [part for part in range(places) if part % 2 == 1]
    even = [part for part in range(places) if part % 2 == 0]
    first_grads, second_grads = [None] * places, [None] * places
    old = ()
    todo = sorted(range(places), key=lambda part: (-abs(2 * part - places), -part))
    todo = [part for part in todo if part != 0] + [0]
    for number in range(0, places, 2):
        group = todo[number : number + 2]
        y_rows, back_rows, in_parts, out_parts = run_experts(
            rows,
            grads,
            [first_all[part] for part in group],
            [second_all[part] for part in group],
            old,
        )
        old = (y_rows, back_rows)
        for part, in_part, out_part in zip(group, in_parts, out_parts):
            first_grads[part], second_grads[part] = in_part, out_part
    in_grad = line_scatter(first_grads, places)
    out_expert_grad = line_scatter(second_grads, places)

    def collect(values, dims_in_order):
        shaped = values.reshape(local_experts, 2, len(keys), capacity, width)
        other = swap(shaped[:, 1], core)
        raw = jnp.einsum("bjst,jbsd->btd", hot_own, shaped[:, 0], preferred_element_type=FULL)
        raw = raw + jnp.einsum("bjst,jbsd->btd", hot_other, other, preferred_element_type=FULL)
        held = {key: raw[number] for number, key in enumerate(keys)}
        return scatter_blocks(held, dims_in_order)

    token_y = collect(y_rows, list(reversed(dims)))
    grad_rows = collect(back_rows, dims)

    mixed = (hidden_one + gate_value[:, None] * token_y).astype(LOW)
    grad_gate = jnp.sum(upstream * token_y, axis=1)
    grad_logits = router_soft * (
        jnp.where(chosen_hot, grad_gate[:, None], 0.0) - (gate_value * grad_gate)[:, None]
    )
    router_local = jnp.dot(normed_two_low.astype(FULL).T, grad_logits, precision=HIGH)
    grad_normed_two = grad_rows + jnp.dot(
        grad_logits, router_full.astype(FULL).T, precision=HIGH
    )
    grad_from_two, gain_grad_two = norm_back(
        hidden_one, inverse_two, gains_float[1], grad_normed_two
    )
    grad_hidden_one = upstream + grad_from_two
    grad_attn_low = grad_hidden_one.astype(LOW)
    out_local = jnp.einsum("td,te->de", attended, grad_attn_low, preferred_element_type=FULL)
    grad_attended = mm(grad_attn_low, out_full, ((1,), (1,)), LOW)
    grad_query, grad_key, grad_value, diagonals = attend_back(projected, grad_attended, probs)
    grad_projected = jnp.concatenate((grad_query, grad_key, grad_value), axis=1)
    qkv_local = jnp.einsum("td,te->de", normed_low, grad_projected, preferred_element_type=FULL)
    grad_normed_one = mm(grad_projected, qkv_full, ((1,), (1,)))
    grad_from_one, gain_grad_one = norm_back(inputs, inverse_one, gains_float[0], grad_normed_one)
    tokens_grad = grad_hidden_one + grad_from_one
    bias_local = jnp.einsum("hrj,rjb->bh", diagonals, bucket_hot, precision=HIGH)
    bias_grad = sum_everywhere(bias_local)
    gains_local = jnp.stack((gain_grad_one, gain_grad_two), axis=1)
    packed_grad = jnp.concatenate(
        (
            qkv_local.astype(LOW),
            out_local.astype(LOW),
            router_local.astype(LOW),
            gains_local.astype(LOW),
            jnp.zeros((width, spare), LOW),
        ),
        axis=1,
    )
    dense_grad = dense_scatter(packed_grad, places, place, dims, core, shard_rows)
    qkv_grad = dense_grad[:, : 3 * width]
    out_grad = dense_grad[:, 3 * width : 4 * width]
    router_grad = dense_grad[:, 4 * width : 4 * width + experts_all]
    gains_grad = dense_grad[:, 4 * width + experts_all : 4 * width + experts_all + 2].T
    return (
        mixed,
        tokens_grad,
        gains_grad,
        qkv_grad,
        out_grad,
        router_grad,
        bias_grad,
        in_grad,
        out_expert_grad,
    )


def solution(mesh):
    rows = P(("fsdp", "dp"), None)
    columns = P(None, ("fsdp", "dp"))
    experts = (P("dp", None, "fsdp"), P("dp", "fsdp", None))
    return jax.shard_map(
        body,
        mesh=mesh,
        in_specs=(rows, rows, rows, rows, columns, rows, rows, rows, P()) + experts,
        out_specs=(rows, rows, columns, rows, rows, rows, P()) + experts,
        check_vma=False,
    )
```

```python
from functools import partial, reduce

import jax
import jax.numpy as jnp
from jax import lax
from jax.experimental import pallas as pl
from jax.experimental.pallas import tpu as pltpu
from jax.sharding import PartitionSpec as P

HEADS = 12
HEAD_DIM = 64
EPS = 1e-06
LIMITS = (12, 16, 23, 32, 46, 64, 91)
SCALE = 0.125
HIGH = lax.Precision.HIGHEST
LOW = jnp.bfloat16
FULL = jnp.float32
ROWS = 128
VMEM_BYTES = 52 * 1024 * 1024


def bucket_index(relative):
    distance = jnp.abs(relative)
    far_bucket = reduce(
        lambda counted, boundary: counted + (distance >= boundary).astype(jnp.int32),
        LIMITS,
        jnp.full_like(distance, 8),
    )
    return jnp.where(distance < 8, distance, far_bucket) + 16 * (relative > 0).astype(jnp.int32)


def segment_ids(lengths, slots):
    ending = jnp.cumsum(lengths)
    places = jnp.arange(slots, dtype=jnp.int32)
    return jnp.sum((places[:, None] >= ending[None, :]).astype(jnp.int32), axis=1)


def rms_parts(values, gain):
    inverse = lax.rsqrt(jnp.mean(values * values, axis=-1, keepdims=True) + EPS)
    return (values * inverse * gain, inverse)


def norm_back(values, inverse, gain, upstream):
    scaled = upstream * gain
    grad_values = inverse * scaled - values * inverse * inverse * inverse * jnp.mean(
        values * scaled, axis=-1, keepdims=True
    )
    return (grad_values, jnp.sum(upstream * values * inverse, axis=0))


def softmax_rows(scores):
    highest = jnp.max(scores, axis=-1, keepdims=True)
    raised = jnp.exp(scores - highest)
    return raised / jnp.sum(raised, axis=-1, keepdims=True)


def mm(left, right, contract, out=FULL):
    return lax.dot_general(left, right, (contract, ((), ())), preferred_element_type=FULL).astype(
        out
    )


def small_cost(flops, bytes_accessed, transcendentals):
    return pl.CostEstimate(
        flops=flops // 64,
        bytes_accessed=bytes_accessed // 64,
        transcendentals=transcendentals // 64,
    )


def nothing_kernel(*refs):
    del refs


def after(values, deps):
    values, deps = list(values), list(deps)
    anywhere = pl.BlockSpec(memory_space=pl.ANY)
    return pl.pallas_call(
        nothing_kernel,
        in_specs=[anywhere] * (len(values) + len(deps)),
        out_specs=[anywhere] * len(values),
        out_shape=[jax.ShapeDtypeStruct(value.shape, value.dtype) for value in values],
        input_output_aliases={number: number for number in range(len(values))},
        name="after",
    )(*values, *deps)


def swap(value, dim):
    axis, mask = dim
    count = lax.axis_size(axis)
    return lax.ppermute(value, axis, [(i, i ^ mask) for i in range(count)])


def bit_of(dim):
    axis, mask = dim
    return (lax.axis_index(axis) & mask) != 0


def stage_pair(value, dim):
    other = swap(value, dim)
    return jnp.where(bit_of(dim), jnp.stack((other, value)), jnp.stack((value, other)))


def ring_shift(value, places, by):
    count = 2 * places
    return lax.ppermute(value, "fsdp", [(i, (i - 2 * by) % count) for i in range(count)])


def z_gather(value, places, place):
    parts = jnp.stack([value] + [ring_shift(value, places, by) for by in range(1, places)])
    return lax.dynamic_slice_in_dim(
        jnp.concatenate((parts, parts)), lax.rem(places - place, places), places, 0
    )


def z_groups(places):
    return [[2 * place + side for place in range(places)] for side in (0, 1)]


def gather_step(held, dim):
    keys = list(held)
    value = jnp.stack([held[key] for key in keys]) if len(keys) > 1 else held[keys[0]]
    return swap(value, dim)


def gather_join(held, dim, arrived):
    keys = list(held)
    joined = dict(held)
    for number, key in enumerate(keys):
        joined[tuple(sorted(key + (dim,)))] = arrived[number] if len(keys) > 1 else arrived
    return joined


def gather_blocks(value, dims):
    held = {(): value}
    for dim in dims:
        held = gather_join(held, dim, gather_step(held, dim))
    return held


def gather_halves(value, dims):
    half = value.shape[0] // 2
    held = [{(): value[:half]}, {(): value[half:]}]
    brought = []
    for number in range(len(dims)):
        steps = (dims[number], dims[len(dims) - 1 - number])
        arrived = [gather_step(part, dim) for part, dim in zip(held, steps)]
        brought.append(arrived)
        held = [gather_join(*of) for of in zip(held, steps, arrived)]
    upper, lower = held
    blocks = jnp.stack([jnp.concatenate((upper[key], lower[key])) for key in sorted(upper)])
    return (blocks, brought)


def scatter_step(held, dim):
    stay = [key for key in held if dim not in key]
    leave = [tuple(sorted(key + (dim,))) for key in stay]
    sent = jnp.stack([held[key].astype(LOW) for key in leave])
    arrived = swap(sent, dim)
    return {
        key: held[key].astype(FULL) + arrived[number].astype(FULL)
        for number, key in enumerate(stay)
    }


def scatter_halves(blocks, keys, dims):
    half = blocks.shape[1] // 2
    upper = {key: blocks[number, :half] for number, key in enumerate(keys)}
    lower = {key: blocks[number, half:] for number, key in enumerate(keys)}
    between = ()
    for number in range(len(dims)):
        upper = scatter_step(upper, dims[len(dims) - 1 - number])
        lower = scatter_step(lower, dims[number])
        if number == 0 and len(dims) > 1:
            upper = {key: value.astype(LOW) for key, value in upper.items()}
            lower = {key: value.astype(LOW) for key, value in lower.items()}
            between = list(upper.values()) + list(lower.values())
    return (jnp.concatenate((upper[()], lower[()])), between)


def dense_gather(value, places, place, dims, core):
    columns = value.shape[1]
    half = (columns // 256) * 128
    near = z_gather(value, places, place)
    wanted = ("z", dims[0]) + tuple(sorted(dims[1:], reverse=True)) + ("core", "rows", "columns")

    def run(part, order):
        axes = ("z", "rows", "columns")
        for dim in order:
            part = stage_pair(part, dim)
            axes = (dim,) + axes
        part = stage_pair(part, core)
        axes = ("core",) + axes
        return part.transpose([axes.index(name) for name in wanted]).reshape(-1, part.shape[-1])

    first = run(near[..., :half], dims)
    second = run(near[..., half:], list(reversed(dims)))
    return (jnp.concatenate((first, second), axis=1), near)


def dense_scatter(value, peer_dims, rows):
    bits = len(peer_dims)
    part = value.reshape((-1,) + (2,) * bits + (rows, value.shape[1]))
    for number, dim in enumerate(peer_dims):
        spot = bits - number
        own = bit_of(dim).astype(jnp.int32)
        keep = lax.dynamic_index_in_dim(part, own, spot, keepdims=False)
        send = lax.dynamic_index_in_dim(part, 1 - own, spot, keepdims=False)
        part = (keep.astype(FULL) + swap(send, dim).astype(FULL)).astype(LOW)
    return part


def dense_finish(part):
    arrived = lax.all_to_all(part, "fsdp", split_axis=0, concat_axis=0, tiled=True)
    return jnp.sum(arrived.astype(FULL), axis=0)


def sum_everywhere(value):
    for axis in ("dp", "fsdp"):
        mask = 1
        while mask < lax.axis_size(axis):
            value = value + swap(value, (axis, mask))
            mask *= 2
    return value


def diagonal_hot(slots, bucket_count):
    width = 2 * slots
    lanes = jnp.arange(width, dtype=jnp.int32)[None, :]
    rows = jnp.arange(8, dtype=jnp.int32)[:, None]
    diagonal = (lanes - rows + (ROWS - 1)) % width
    bucket = jnp.where(diagonal < width - 1, bucket_index(diagonal - (slots - 1)), -1)
    return (bucket[:, :, None] == jnp.arange(bucket_count, dtype=jnp.int32)).astype(FULL)


def attend_kernel(query, key, value, base, seg_col, seg_row, out, probs, toeplitz):
    slots = query.shape[0]
    lanes = lax.broadcasted_iota(jnp.int32, (1, 2 * HEAD_DIM), 1)
    total = [None] * (slots // ROWS)
    for head in range(2):
        mine = (lanes >= head * HEAD_DIM) & (lanes < (head + 1) * HEAD_DIM)
        table = base[head]
        size = 8
        while size < ROWS:
            table = jnp.concatenate((table, pltpu.roll(table, size, 1)), axis=0)
            size *= 2
        toeplitz[...] = table
        value_head = jnp.where(mine, value[...], 0).astype(LOW)
        for block in range(slots // ROWS):
            rows = pl.ds(block * ROWS, ROWS)
            query_head = jnp.where(mine, query[rows, :], 0).astype(LOW)
            shift = slots - ROWS - block * ROWS
            scores = mm(query_head, key[...], ((1,), (1,))) * SCALE
            scores = scores + toeplitz[:, shift : shift + slots]
            scores = jnp.where(seg_col[rows, :] == seg_row[...], scores, -1e30)
            highest = jnp.max(scores, axis=-1, keepdims=True)
            raised = jnp.exp(scores - highest)
            low = (raised / jnp.sum(raised, axis=-1, keepdims=True)).astype(LOW)
            probs[head, rows, :] = low
            part = mm(low, value_head, ((1,), (0,)))
            total[block] = part if head == 0 else total[block] + part
    for block in range(slots // ROWS):
        out[pl.ds(block * ROWS, ROWS), :] = total[block].astype(LOW)


def attend_forward(projected, base, seg_col, seg_row):
    slots = projected.shape[0]
    width = projected.shape[1] // 3
    pairs = HEADS // 2
    lanes = 2 * HEAD_DIM
    return pl.pallas_call(
        attend_kernel,
        grid=(pairs,),
        in_specs=[
            pl.BlockSpec((slots, lanes), lambda p: (0, p)),
            pl.BlockSpec((slots, lanes), lambda p: (0, p + pairs)),
            pl.BlockSpec((slots, lanes), lambda p: (0, p + 2 * pairs)),
            pl.BlockSpec((2, 8, 2 * slots), lambda p: (p, 0, 0)),
            pl.BlockSpec((slots, 1), lambda p: (0, 0)),
            pl.BlockSpec((1, slots), lambda p: (0, 0)),
        ],
        out_specs=[
            pl.BlockSpec((slots, lanes), lambda p: (0, p)),
            pl.BlockSpec((2, slots, slots), lambda p: (p, 0, 0)),
        ],
        out_shape=[
            jax.ShapeDtypeStruct((slots, width), LOW),
            jax.ShapeDtypeStruct((HEADS, slots, slots), LOW),
        ],
        scratch_shapes=[pltpu.VMEM((ROWS, 2 * slots), FULL)],
        compiler_params=pltpu.CompilerParams(vmem_limit_bytes=VMEM_BYTES),
        cost_estimate=small_cost(
            flops=HEADS * slots * slots * HEAD_DIM * 16,
            bytes_accessed=HEADS * slots * slots * 2 + 8 * slots * width,
            transcendentals=HEADS * slots * slots,
        ),
        name="attend_forward",
    )(projected, projected, projected, base, seg_col, seg_row)


def attend_back_kernel(
    query, key, value, grad, probs, out_query, out_key, out_value, diagonals, lined, scores_low
):
    slots = query.shape[0]
    lanes = lax.broadcasted_iota(jnp.int32, (1, 2 * HEAD_DIM), 1)
    query_total = [None] * (slots // ROWS)
    key_total = value_total = None
    for head in range(2):
        mine = (lanes >= head * HEAD_DIM) & (lanes < (head + 1) * HEAD_DIM)
        key_head = jnp.where(mine, key[...], 0).astype(LOW)
        grad_head = jnp.where(mine, grad[...], 0).astype(LOW)
        query_head = jnp.where(mine, query[...], 0).astype(LOW)
        lined[...] = jnp.zeros_like(lined)
        for block in range(slots // ROWS):
            rows = pl.ds(block * ROWS, ROWS)
            soft = probs[head, rows, :].astype(FULL)
            grad_rows = jnp.where(mine, grad[rows, :], 0).astype(LOW)
            weighted = soft * mm(grad_rows, value[...], ((1,), (1,)))
            back = weighted - soft * jnp.sum(weighted, axis=-1, keepdims=True)
            low = back.astype(LOW)
            scores_low[rows, :] = low
            shift = slots - ROWS - block * ROWS
            lined[:, shift : shift + slots] += low.astype(FULL)
            part = mm(low, key_head, ((1,), (0,)))
            query_total[block] = part if head == 0 else query_total[block] + part
        key_part = mm(scores_low[...], query_head, ((0,), (0,)))
        value_part = mm(probs[head], grad_head, ((0,), (0,)))
        key_total = key_part if head == 0 else key_total + key_part
        value_total = value_part if head == 0 else value_total + value_part
        table = lined[...]
        size = ROWS
        while size > 8:
            size //= 2
            table = table[:size] + pltpu.roll(table[size:], 2 * slots - size, 1)
        diagonals[head] = table
    out_key[...] = (key_total * SCALE).astype(LOW)
    out_value[...] = value_total.astype(LOW)
    for block in range(slots // ROWS):
        out_query[pl.ds(block * ROWS, ROWS), :] = (query_total[block] * SCALE).astype(LOW)


def attend_back(projected, grad_attended, probs, begin, count):
    slots = projected.shape[0]
    pairs = HEADS // 2
    lanes = 2 * HEAD_DIM
    width = count * lanes
    column = pl.BlockSpec((slots, lanes), lambda p: (0, p))

    def column_from(offset):
        return pl.BlockSpec((slots, lanes), lambda p: (0, p + offset))

    return pl.pallas_call(
        attend_back_kernel,
        grid=(count,),
        in_specs=[
            column_from(begin),
            column_from(begin + pairs),
            column_from(begin + 2 * pairs),
            column_from(begin),
            pl.BlockSpec((2, slots, slots), lambda p: (p + begin, 0, 0)),
        ],
        out_specs=[
            column,
            column,
            column,
            pl.BlockSpec((2, 8, 2 * slots), lambda p: (p, 0, 0)),
        ],
        out_shape=[jax.ShapeDtypeStruct((slots, width), LOW)] * 3
        + [jax.ShapeDtypeStruct((2 * count, 8, 2 * slots), FULL)],
        scratch_shapes=[pltpu.VMEM((ROWS, 2 * slots), FULL), pltpu.VMEM((slots, slots), LOW)],
        compiler_params=pltpu.CompilerParams(vmem_limit_bytes=VMEM_BYTES),
        cost_estimate=small_cost(
            flops=2 * count * slots * slots * HEAD_DIM * 32,
            bytes_accessed=2 * count * slots * slots * 2 + 14 * slots * width,
            transcendentals=0,
        ),
        name="attend_back",
    )(projected, projected, projected, grad_attended, probs)


def expert_forward_kernel(rows, first, second, y_out, hidden_out, slope_out, y_sum):
    chunk = pl.program_id(0)
    count = rows.shape[1]
    step = min(256, count)

    @pl.when(chunk == 0)
    def _():
        y_sum[...] = jnp.zeros_like(y_sum)

    for block in range(count // step):
        some = pl.ds(block * step, step)
        pre = mm(rows[0, some, :], first[0], ((1,), (0,)))
        normal_cdf = 0.5 + 0.5 * lax.erf(pre * 0.7071067811865476)
        slope = normal_cdf + pre * jnp.exp(-0.5 * pre * pre) * 0.3989422804014327
        hidden = (pre * normal_cdf).astype(LOW)
        hidden_out[0, some, :] = hidden
        slope_out[0, some, :] = slope.astype(LOW)
        y_sum[some, :] += mm(hidden, second[0], ((1,), (0,)))

    @pl.when(chunk == pl.num_programs(0) - 1)
    def _():
        y_out[...] = y_sum[...].astype(LOW)


def expert_specs(expert, count, width, units):
    def part(*shape):
        return pl.BlockSpec((1,) + shape, lambda c: (c, 0, 0))

    rows_in = pl.BlockSpec((1, count, width), lambda c: (expert, 0, 0))
    rows_out = pl.BlockSpec((count, width), lambda c: (0, 0))
    return (rows_in, rows_out, part(width, units), part(units, width), part(count, units))


def expert_forward(expert, rows, first, second):
    chunks, width, units = first.shape
    count = rows.shape[1]
    rows_in, rows_out, first_spec, second_spec, unit_spec = expert_specs(expert, count, width, units)
    hidden_shape = jax.ShapeDtypeStruct((chunks, count, units), LOW)
    return pl.pallas_call(
        expert_forward_kernel,
        grid=(chunks,),
        in_specs=[rows_in, first_spec, second_spec],
        out_specs=[rows_out, unit_spec, unit_spec],
        out_shape=[jax.ShapeDtypeStruct((count, width), LOW), hidden_shape, hidden_shape],
        scratch_shapes=[pltpu.VMEM((count, width), FULL)],
        compiler_params=pltpu.CompilerParams(vmem_limit_bytes=VMEM_BYTES),
        cost_estimate=small_cost(
            flops=chunks * 4 * count * width * units,
            bytes_accessed=4 * count * width + 4 * chunks * (width + count) * units,
            transcendentals=2 * chunks * count * units,
        ),
        name="expert_forward",
    )(rows, first, second)


def expert_back_kernel(
    rows, grads, first, second, hidden, slope, back_out, first_out, second_out, back_sum, pre_low
):
    chunk = pl.program_id(0)
    count = rows.shape[1]
    step = min(256, count)

    @pl.when(chunk == 0)
    def _():
        back_sum[...] = jnp.zeros_like(back_sum)

    for block in range(count // step):
        some = pl.ds(block * step, step)
        grad_hidden = mm(grads[0, some, :], second[0], ((1,), (1,)))
        grad_pre = (grad_hidden * slope[0, some, :].astype(FULL)).astype(LOW)
        pre_low[some, :] = grad_pre
        back_sum[some, :] += mm(grad_pre, first[0], ((1,), (1,)))
    first_out[0] = mm(rows[0], pre_low[...], ((0,), (0,)), LOW)
    second_out[0] = mm(hidden[0], grads[0], ((0,), (0,)), LOW)

    @pl.when(chunk == pl.num_programs(0) - 1)
    def _():
        back_out[...] = back_sum[...].astype(LOW)


def expert_back(expert, rows, grads, first, second, hidden, slope):
    chunks, width, units = first.shape
    count = rows.shape[1]
    rows_in, rows_out, first_spec, second_spec, unit_spec = expert_specs(expert, count, width, units)
    return pl.pallas_call(
        expert_back_kernel,
        grid=(chunks,),
        in_specs=[rows_in, rows_in, first_spec, second_spec, unit_spec, unit_spec],
        out_specs=[rows_out, first_spec, second_spec],
        out_shape=[
            jax.ShapeDtypeStruct((count, width), LOW),
            jax.ShapeDtypeStruct(first.shape, LOW),
            jax.ShapeDtypeStruct(second.shape, LOW),
        ],
        scratch_shapes=[pltpu.VMEM((count, width), FULL), pltpu.VMEM((count, units), LOW)],
        compiler_params=pltpu.CompilerParams(vmem_limit_bytes=VMEM_BYTES),
        cost_estimate=small_cost(
            flops=chunks * 8 * count * width * units,
            bytes_accessed=6 * count * width + 4 * chunks * (2 * width + count) * units,
            transcendentals=0,
        ),
        name="expert_back",
    )(rows, grads, first, second, hidden, slope)


def body(
    tokens,
    cotangent,
    seq_lens,
    routes,
    norm_gains,
    qkv_weight,
    out_weight,
    router_weight,
    rel_bias,
    expert_in,
    expert_out,
):
    tok_count, width = tokens.shape
    bucket_count = rel_bias.shape[0]
    shard_rows = qkv_weight.shape[0]
    experts_all = router_weight.shape[1]
    local_experts = expert_in.shape[0]
    capacity = 2 * tok_count // experts_all
    places = lax.axis_size("fsdp") // 2
    place = lax.axis_index("fsdp") // 2
    peer = lax.axis_index("dp")
    peer_count = lax.axis_size("dp")
    core = ("dp", 1)
    dims = [("fsdp", 1)]
    mask = 2
    while mask < peer_count:
        dims.append(("dp", mask))
        mask *= 2

    spare = -(4 * width + experts_all + 2) % 128
    packed = jnp.concatenate(
        (
            qkv_weight,
            out_weight,
            router_weight,
            norm_gains.T,
            jnp.zeros((shard_rows, spare), LOW),
        ),
        axis=1,
    )
    dense, near = dense_gather(packed, places, place, dims, core)
    qkv_full = dense[:, : 3 * width]
    out_full = dense[:, 3 * width : 4 * width]
    router_full = dense[:, 4 * width : 4 * width + experts_all]
    gains_float = dense[:, 4 * width + experts_all : 4 * width + experts_all + 2].T.astype(FULL)

    groups = z_groups(places)
    weights = []
    for expert in range(local_experts):
        own = (expert_in[expert], expert_out[expert])
        if expert > 0:
            own = after(own, (near,))
        weights.append([lax.all_gather(v, "fsdp", axis=0, axis_index_groups=groups) for v in own])

    chosen = routes[:, 0]
    chosen_hot = chosen[:, None] == jnp.arange(experts_all, dtype=jnp.int32)[None, :]
    order = jnp.arange(tok_count, dtype=jnp.int32)
    earlier = (order[:, None] > order[None, :]).astype(LOW)
    rank_all = jnp.dot(earlier, chosen_hot.astype(LOW), preferred_element_type=FULL)
    rank_in = jnp.sum(jnp.where(chosen_hot, rank_all, 0.0), axis=1).astype(jnp.int32)
    slots_of = gather_blocks((chosen * capacity + rank_in)[None, :], dims)
    keys = sorted(slots_of)
    slots_near = jnp.stack([slots_of[key][0] for key in keys])
    local_slots = local_experts * capacity
    slot_ids = jnp.arange(local_slots, dtype=jnp.int32).reshape(local_experts, capacity)

    def hot_of(owner):
        wanted = owner * local_slots + slot_ids
        return (slots_near[:, None, None, :] == wanted[None, :, :, None]).astype(LOW)

    hot_own, hot_other = hot_of(peer), hot_of(peer ^ 1)
    segment = segment_ids(seq_lens[0], tok_count)
    bucket_hot = diagonal_hot(tok_count, bucket_count)
    base = jnp.einsum("rjb,bh->hrj", bucket_hot, rel_bias, precision=HIGH)

    inputs = tokens.astype(FULL)
    normed_one, inverse_one = rms_parts(inputs, gains_float[0])
    normed_low = normed_one.astype(LOW)
    projected = jnp.dot(normed_low, qkv_full, preferred_element_type=FULL).astype(LOW)
    attended, probs = attend_forward(projected, base, segment[:, None], segment[None, :])
    hidden_one = inputs + jnp.dot(attended, out_full, preferred_element_type=FULL)
    normed_two, inverse_two = rms_parts(hidden_one, gains_float[1])
    normed_two_low = normed_two.astype(LOW)
    router_soft = softmax_rows(jnp.dot(normed_two_low, router_full, preferred_element_type=FULL))
    gate_value = jnp.sum(jnp.where(chosen_hot, router_soft, 0.0), axis=1)
    upstream = cotangent.astype(FULL)
    grad_y = (gate_value[:, None] * upstream).astype(LOW)

    def pick(hot, blocks):
        return jnp.einsum("bjst,btd->jbsd", hot, blocks, preferred_element_type=FULL).astype(LOW)

    def to_rows(blocks):
        other = swap(pick(hot_other, blocks), core)
        both = jnp.stack((pick(hot_own, blocks), other), axis=1)
        return both.reshape(local_experts, -1, width)

    hot_all = jnp.concatenate((hot_own, hot_other), axis=1).reshape(
        len(keys), 2 * local_slots, tok_count
    )

    def from_rows(values, ready=()):
        shaped = [value.reshape(2, len(keys), capacity, width) for value in values]
        parts = [part[0] for part in shaped] + [swap(part[1], core) for part in shaped]
        joined = jnp.concatenate(parts, axis=1)
        if ready:
            (joined,) = after((joined,), ready)
        return jnp.einsum("bst,bsd->btd", hot_all, joined, preferred_element_type=FULL).astype(LOW)

    blocks, brought = gather_halves(normed_two_low, dims)
    rows = to_rows(blocks)
    grad_half = tok_count // 2
    grad_parts = after((grad_y[:grad_half], grad_y[grad_half:]), brought[0])
    held = [{(): part} for part in grad_parts]
    grad_brought = []
    forwards = []
    for number in range(len(dims)):
        steps = (dims[number], dims[len(dims) - 1 - number])
        arrived = [gather_step(part, dim) for part, dim in zip(held, steps)]
        if number == len(dims) - 1:
            (tied,) = after((rows,), sum(grad_brought, []))
            forwards.append(expert_forward(0, tied, *weights[0]))
            arrived = after(arrived, (forwards[0][0],))
        grad_brought.append(arrived)
        held = [gather_join(*of) for of in zip(held, steps, arrived)]
    grad_blocks = jnp.stack(
        [jnp.concatenate((held[0][key], held[1][key])) for key in sorted(held[0])]
    )
    grads = to_rows(grad_blocks)
    backs = []
    for expert in range(local_experts):
        if expert > 0:
            (tied,) = after((rows,), (backs[-1][0],))
            forwards.append(expert_forward(expert, tied, *weights[expert]))
        tied = grads
        if expert == local_experts - 1:
            y_raw = from_rows([forward[0] for forward in forwards])
            token_y, y_between = scatter_halves(y_raw, keys, dims)
            (tied,) = after((grads,), (y_raw,))
        backs.append(expert_back(expert, rows, tied, *weights[expert], *forwards[expert][1:]))
    in_grad, out_expert_grad = (
        jnp.stack(
            [
                lax.psum_scatter(
                    back[which], "fsdp", scatter_dimension=0, axis_index_groups=groups, tiled=False
                ).astype(FULL)
                for back in backs
            ]
        )
        for which in (1, 2)
    )
    grad_rows, _ = scatter_halves(
        from_rows([back[0] for back in backs], y_between), keys, dims
    )

    mixed = (hidden_one + gate_value[:, None] * token_y).astype(LOW)
    grad_gate = jnp.sum(upstream * token_y, axis=1)
    grad_logits = router_soft * (
        jnp.where(chosen_hot, grad_gate[:, None], 0.0) - (gate_value * grad_gate)[:, None]
    )
    router_local = jnp.dot(normed_two_low.astype(FULL).T, grad_logits, precision=HIGH)
    grad_normed_two = grad_rows + jnp.dot(
        grad_logits, router_full.astype(FULL).T, precision=HIGH
    )
    grad_from_two, gain_grad_two = norm_back(
        hidden_one, inverse_two, gains_float[1], grad_normed_two
    )
    grad_hidden_one = upstream + grad_from_two
    grad_attn_low = grad_hidden_one.astype(LOW)
    out_local = jnp.einsum("td,te->de", attended, grad_attn_low, preferred_element_type=FULL)
    grad_attended = mm(grad_attn_low, out_full, ((1,), (1,)), LOW)
    peer_dims = [core] + dims[1:]
    spare_out = -(experts_all + 2) % 128
    out_panel = jnp.concatenate(
        (
            out_local.astype(LOW),
            router_local.astype(LOW),
            gain_grad_two[:, None].astype(LOW),
            jnp.zeros((width, spare_out + 1), LOW),
        ),
        axis=1,
    )
    (grad_attended,) = after((grad_attended,), (out_panel,))
    out_part = dense_scatter(out_panel, peer_dims, shard_rows)
    pairs = HEADS // 2
    halves = ((0, pairs // 2), (pairs // 2, pairs - pairs // 2))
    grad_normed_one = 0.0
    diagonals, sums = [], []
    for number, (begin, count) in enumerate(halves):
        if number > 0:
            (grad_attended,) = after((grad_attended,), (panel, out_part))
        *grad_parts, lined = attend_back(projected, grad_attended, probs, begin, count)
        diagonals.append(lined)
        piece = jnp.concatenate(grad_parts, axis=1)
        lanes = count * 2 * HEAD_DIM
        weight = jnp.concatenate(
            [
                qkv_full[:, width * part + begin * 2 * HEAD_DIM :][:, :lanes]
                for part in range(3)
            ],
            axis=1,
        )
        grad_normed_one = grad_normed_one + mm(piece, weight, ((1,), (1,)))
        qkv_local = jnp.einsum("td,te->de", normed_low, piece, preferred_element_type=FULL)
        panel = qkv_local.astype(LOW)
        sums.append(dense_scatter(panel, peer_dims, shard_rows))
    out_sum = dense_finish(out_part)
    last_sum = dense_finish(jnp.concatenate(sums, axis=-1))
    starts = [0] + [3 * count * 2 * HEAD_DIM for _, count in halves][:-1]
    sums = [last_sum[:, start:] for start in starts]
    grad_from_one, gain_grad_one = norm_back(inputs, inverse_one, gains_float[0], grad_normed_one)
    tokens_grad = grad_hidden_one + grad_from_one
    bias_local = jnp.einsum(
        "hrj,rjb->bh", jnp.concatenate(diagonals), bucket_hot, precision=HIGH
    )
    gain_rows = width // 128
    small = jnp.concatenate((bias_local.reshape(-1, 128), gain_grad_one.reshape(-1, 128)))
    small = sum_everywhere(small)
    bias_grad = small[:-gain_rows].reshape(bias_local.shape)
    device = lax.axis_index("fsdp") * peer_count + peer
    gain_one = lax.dynamic_slice_in_dim(
        small[-gain_rows:].reshape(-1), device * shard_rows, shard_rows
    )
    gains_grad = jnp.stack((gain_one, out_sum[:, width + experts_all]))
    router_grad = out_sum[:, width : width + experts_all]
    out_grad = out_sum[:, :width]
    qkv_grad = jnp.concatenate(
        [
            sums[number][:, part * count * 2 * HEAD_DIM :][:, : count * 2 * HEAD_DIM]
            for part in range(3)
            for number, (_, count) in enumerate(halves)
        ],
        axis=1,
    )
    return (
        mixed,
        tokens_grad,
        gains_grad,
        qkv_grad,
        out_grad,
        router_grad,
        bias_grad,
        in_grad,
        out_expert_grad,
    )


def solution(mesh):
    rows = P(("fsdp", "dp"), None)
    columns = P(None, ("fsdp", "dp"))
    experts = (P("dp", None, "fsdp"), P("dp", "fsdp", None))
    return jax.shard_map(
        body,
        mesh=mesh,
        in_specs=(rows, rows, rows, rows, columns, rows, rows, rows, P()) + experts,
        out_specs=(rows, rows, columns, rows, rows, rows, P()) + experts,
        check_vma=False,
    )
```

```python
from functools import partial, reduce

import jax
import jax.numpy as jnp
from jax import lax
from jax.experimental import pallas as pl
from jax.experimental.pallas import tpu as pltpu
from jax.sharding import PartitionSpec as P

HEADS = 12
HEAD_DIM = 64
EPS = 1e-06
LIMITS = (12, 16, 23, 32, 46, 64, 91)
SCALE = 0.125
HIGH = lax.Precision.HIGHEST
LOW = jnp.bfloat16
FULL = jnp.float32
ROWS = 128
VMEM_BYTES = 52 * 1024 * 1024


def bucket_index(relative):
    distance = jnp.abs(relative)
    far_bucket = reduce(
        lambda counted, boundary: counted + (distance >= boundary).astype(jnp.int32),
        LIMITS,
        jnp.full_like(distance, 8),
    )
    return jnp.where(distance < 8, distance, far_bucket) + 16 * (relative > 0).astype(jnp.int32)


def segment_ids(lengths, slots):
    ending = jnp.cumsum(lengths)
    places = jnp.arange(slots, dtype=jnp.int32)
    return jnp.sum((places[:, None] >= ending[None, :]).astype(jnp.int32), axis=1)


def rms_parts(values, gain):
    inverse = lax.rsqrt(jnp.mean(values * values, axis=-1, keepdims=True) + EPS)
    return (values * inverse * gain, inverse)


def norm_back(values, inverse, gain, upstream):
    scaled = upstream * gain
    grad_values = inverse * scaled - values * inverse * inverse * inverse * jnp.mean(
        values * scaled, axis=-1, keepdims=True
    )
    return (grad_values, jnp.sum(upstream * values * inverse, axis=0))


def softmax_rows(scores):
    highest = jnp.max(scores, axis=-1, keepdims=True)
    raised = jnp.exp(scores - highest)
    return raised / jnp.sum(raised, axis=-1, keepdims=True)


def mm(left, right, contract, out=FULL):
    return lax.dot_general(left, right, (contract, ((), ())), preferred_element_type=FULL).astype(
        out
    )


def small_cost(flops, bytes_accessed, transcendentals):
    return pl.CostEstimate(
        flops=flops // 64,
        bytes_accessed=bytes_accessed // 64,
        transcendentals=transcendentals // 64,
    )


def nothing_kernel(*refs):
    del refs


def after(values, deps):
    values, deps = list(values), list(deps)
    anywhere = pl.BlockSpec(memory_space=pl.ANY)
    return pl.pallas_call(
        nothing_kernel,
        in_specs=[anywhere] * (len(values) + len(deps)),
        out_specs=[anywhere] * len(values),
        out_shape=[jax.ShapeDtypeStruct(value.shape, value.dtype) for value in values],
        input_output_aliases={number: number for number in range(len(values))},
        name="after",
    )(*values, *deps)


def swap(value, dim):
    axis, mask = dim
    count = lax.axis_size(axis)
    return lax.ppermute(value, axis, [(i, i ^ mask) for i in range(count)])


def bit_of(dim):
    axis, mask = dim
    return (lax.axis_index(axis) & mask) != 0


def stage_pair(value, dim):
    other = swap(value, dim)
    return jnp.where(bit_of(dim), jnp.stack((other, value)), jnp.stack((value, other)))


def ring_shift(value, places, by):
    count = 2 * places
    return lax.ppermute(value, "fsdp", [(i, (i - 2 * by) % count) for i in range(count)])


def z_gather(value, places, place):
    parts = jnp.stack([value] + [ring_shift(value, places, by) for by in range(1, places)])
    return lax.dynamic_slice_in_dim(
        jnp.concatenate((parts, parts)), lax.rem(places - place, places), places, 0
    )


def z_groups(places):
    return [[2 * place + side for place in range(places)] for side in (0, 1)]


def gather_step(held, dim):
    keys = list(held)
    value = jnp.stack([held[key] for key in keys]) if len(keys) > 1 else held[keys[0]]
    return swap(value, dim)


def gather_join(held, dim, arrived):
    keys = list(held)
    joined = dict(held)
    for number, key in enumerate(keys):
        joined[tuple(sorted(key + (dim,)))] = arrived[number] if len(keys) > 1 else arrived
    return joined


def gather_blocks(value, dims):
    held = {(): value}
    for dim in dims:
        held = gather_join(held, dim, gather_step(held, dim))
    return held


def gather_halves(value, dims):
    half = value.shape[0] // 2
    held = [{(): value[:half]}, {(): value[half:]}]
    brought = []
    for number in range(len(dims)):
        steps = (dims[number], dims[len(dims) - 1 - number])
        arrived = after([gather_step(part, dim) for part, dim in zip(held, steps)], ())
        brought.append(arrived)
        held = [gather_join(*of) for of in zip(held, steps, arrived)]
    upper, lower = held
    blocks = jnp.stack([jnp.concatenate((upper[key], lower[key])) for key in sorted(upper)])
    return (blocks, brought)


def scatter_halves(blocks, keys, dims):
    half = blocks.shape[1] // 2
    parts = [
        {key: blocks[number, :half] for number, key in enumerate(keys)},
        {key: blocks[number, half:] for number, key in enumerate(keys)},
    ]
    for number in range(len(dims)):
        steps = (dims[len(dims) - 1 - number], dims[number])
        stay = [[key for key in held if dim not in key] for held, dim in zip(parts, steps)]
        sent = [
            jnp.stack([held[tuple(sorted(key + (dim,)))].astype(LOW) for key in some])
            for held, dim, some in zip(parts, steps, stay)
        ]
        arrived = after([swap(value, dim) for value, dim in zip(sent, steps)], ())
        parts = [
            {
                key: held[key].astype(FULL) + value[place].astype(FULL)
                for place, key in enumerate(some)
            }
            for held, value, some in zip(parts, arrived, stay)
        ]
    return jnp.concatenate((parts[0][()], parts[1][()]))


def dense_gather(value, places, place, dims, core):
    columns = value.shape[1]
    half = (columns // 256) * 128
    near = z_gather(value, places, place)
    wanted = ("z", dims[0]) + tuple(sorted(dims[1:], reverse=True)) + ("core", "rows", "columns")

    def run(part, order):
        axes = ("z", "rows", "columns")
        for dim in order:
            part = stage_pair(part, dim)
            axes = (dim,) + axes
        part = stage_pair(part, core)
        axes = ("core",) + axes
        return part.transpose([axes.index(name) for name in wanted]).reshape(-1, part.shape[-1])

    first = run(near[..., :half], dims)
    second = run(near[..., half:], list(reversed(dims)))
    return (jnp.concatenate((first, second), axis=1), near)


def halve(parts, all_names, dims, beside=()):
    kept, sent, left = [], [], []
    for part, names, dim in zip(parts, all_names, dims):
        spot = names.index(dim)
        own = bit_of(dim).astype(jnp.int32)
        kept.append(lax.dynamic_index_in_dim(part, own, spot, keepdims=False))
        send = lax.dynamic_index_in_dim(part, 1 - own, spot, keepdims=False)
        sent.append(swap(send, dim))
        left.append(names[:spot] + names[spot + 1 :])
    arrived = after(sent + list(beside), ())
    sums = [(a.astype(FULL) + b.astype(FULL)).astype(LOW) for a, b in zip(kept, arrived)]
    return (sums, left, arrived[len(sent) :])


def dense_scatter(parts, names, orders, places, place, small, small_dims):
    all_names = [names] * len(parts)
    for dims, dim in zip(zip(*orders), small_dims):
        parts, all_names, (other,) = halve(parts, all_names, dims, (swap(small, dim),))
        small = small + other
    moved = []
    for part in parts:
        for by in range(1, places):
            send = lax.dynamic_index_in_dim(part, lax.rem(place + by, places), 0, keepdims=False)
            moved.append(ring_shift(send, places, places - by))
    *moved, other = after(moved + [swap(small, small_dims[-1])], ())
    small = small + other
    small = reduce(
        lambda total, by: total + ring_shift(small, places, by), range(1, places), small
    )
    count = places - 1
    sums = [
        reduce(
            lambda total, value: total + value.astype(FULL),
            moved[number * count : (number + 1) * count],
            lax.dynamic_index_in_dim(part, place, 0, keepdims=False).astype(FULL),
        )
        for number, part in enumerate(parts)
    ]
    return (sums, small)


def diagonal_hot(slots, bucket_count):
    width = 2 * slots
    lanes = jnp.arange(width, dtype=jnp.int32)[None, :]
    rows = jnp.arange(8, dtype=jnp.int32)[:, None]
    diagonal = (lanes - rows + (ROWS - 1)) % width
    bucket = jnp.where(diagonal < width - 1, bucket_index(diagonal - (slots - 1)), -1)
    return (bucket[:, :, None] == jnp.arange(bucket_count, dtype=jnp.int32)).astype(FULL)


def attend_kernel(query, key, value, base, seg_col, seg_row, out, probs, toeplitz):
    slots = query.shape[0]
    lanes = lax.broadcasted_iota(jnp.int32, (1, 2 * HEAD_DIM), 1)
    total = [None] * (slots // ROWS)
    for head in range(2):
        mine = (lanes >= head * HEAD_DIM) & (lanes < (head + 1) * HEAD_DIM)
        table = base[head]
        size = 8
        while size < ROWS:
            table = jnp.concatenate((table, pltpu.roll(table, size, 1)), axis=0)
            size *= 2
        toeplitz[...] = table
        value_head = jnp.where(mine, value[...], 0).astype(LOW)
        for block in range(slots // ROWS):
            rows = pl.ds(block * ROWS, ROWS)
            query_head = jnp.where(mine, query[rows, :], 0).astype(LOW)
            shift = slots - ROWS - block * ROWS
            scores = mm(query_head, key[...], ((1,), (1,))) * SCALE
            scores = scores + toeplitz[:, shift : shift + slots]
            scores = jnp.where(seg_col[rows, :] == seg_row[...], scores, -1e30)
            highest = jnp.max(scores, axis=-1, keepdims=True)
            raised = jnp.exp(scores - highest)
            low = (raised / jnp.sum(raised, axis=-1, keepdims=True)).astype(LOW)
            probs[head, rows, :] = low
            part = mm(low, value_head, ((1,), (0,)))
            total[block] = part if head == 0 else total[block] + part
    for block in range(slots // ROWS):
        out[pl.ds(block * ROWS, ROWS), :] = total[block].astype(LOW)


def attend_forward(projected, base, seg_col, seg_row):
    slots = projected.shape[0]
    width = projected.shape[1] // 3
    pairs = HEADS // 2
    lanes = 2 * HEAD_DIM
    return pl.pallas_call(
        attend_kernel,
        grid=(pairs,),
        in_specs=[
            pl.BlockSpec((slots, lanes), lambda p: (0, p)),
            pl.BlockSpec((slots, lanes), lambda p: (0, p + pairs)),
            pl.BlockSpec((slots, lanes), lambda p: (0, p + 2 * pairs)),
            pl.BlockSpec((2, 8, 2 * slots), lambda p: (p, 0, 0)),
            pl.BlockSpec((slots, 1), lambda p: (0, 0)),
            pl.BlockSpec((1, slots), lambda p: (0, 0)),
        ],
        out_specs=[
            pl.BlockSpec((slots, lanes), lambda p: (0, p)),
            pl.BlockSpec((2, slots, slots), lambda p: (p, 0, 0)),
        ],
        out_shape=[
            jax.ShapeDtypeStruct((slots, width), LOW),
            jax.ShapeDtypeStruct((HEADS, slots, slots), LOW),
        ],
        scratch_shapes=[pltpu.VMEM((ROWS, 2 * slots), FULL)],
        compiler_params=pltpu.CompilerParams(vmem_limit_bytes=VMEM_BYTES),
        cost_estimate=small_cost(
            flops=HEADS * slots * slots * HEAD_DIM * 16,
            bytes_accessed=HEADS * slots * slots * 2 + 8 * slots * width,
            transcendentals=HEADS * slots * slots,
        ),
        name="attend_forward",
    )(projected, projected, projected, base, seg_col, seg_row)


def attend_back_kernel(
    query, key, value, grad, probs, out_query, out_key, out_value, diagonals, lined, scores_low
):
    slots = query.shape[0]
    lanes = lax.broadcasted_iota(jnp.int32, (1, 2 * HEAD_DIM), 1)
    query_total = [None] * (slots // ROWS)
    key_total = value_total = None
    for head in range(2):
        mine = (lanes >= head * HEAD_DIM) & (lanes < (head + 1) * HEAD_DIM)
        key_head = jnp.where(mine, key[...], 0).astype(LOW)
        grad_head = jnp.where(mine, grad[...], 0).astype(LOW)
        query_head = jnp.where(mine, query[...], 0).astype(LOW)
        lined[...] = jnp.zeros_like(lined)
        for block in range(slots // ROWS):
            rows = pl.ds(block * ROWS, ROWS)
            soft = probs[head, rows, :].astype(FULL)
            grad_rows = jnp.where(mine, grad[rows, :], 0).astype(LOW)
            weighted = soft * mm(grad_rows, value[...], ((1,), (1,)))
            back = weighted - soft * jnp.sum(weighted, axis=-1, keepdims=True)
            low = back.astype(LOW)
            scores_low[rows, :] = low
            shift = slots - ROWS - block * ROWS
            lined[:, shift : shift + slots] += low.astype(FULL)
            part = mm(low, key_head, ((1,), (0,)))
            query_total[block] = part if head == 0 else query_total[block] + part
        key_part = mm(scores_low[...], query_head, ((0,), (0,)))
        value_part = mm(probs[head], grad_head, ((0,), (0,)))
        key_total = key_part if head == 0 else key_total + key_part
        value_total = value_part if head == 0 else value_total + value_part
        table = lined[...]
        size = ROWS
        while size > 8:
            size //= 2
            table = table[:size] + pltpu.roll(table[size:], 2 * slots - size, 1)
        diagonals[head] = table
    out_key[...] = (key_total * SCALE).astype(LOW)
    out_value[...] = value_total.astype(LOW)
    for block in range(slots // ROWS):
        out_query[pl.ds(block * ROWS, ROWS), :] = (query_total[block] * SCALE).astype(LOW)


def attend_back(projected, grad_attended, probs, begin, count):
    slots = projected.shape[0]
    pairs = HEADS // 2
    lanes = 2 * HEAD_DIM
    width = count * lanes
    column = pl.BlockSpec((slots, lanes), lambda p: (0, p))

    def column_from(offset):
        return pl.BlockSpec((slots, lanes), lambda p: (0, p + offset))

    return pl.pallas_call(
        attend_back_kernel,
        grid=(count,),
        in_specs=[
            column_from(begin),
            column_from(begin + pairs),
            column_from(begin + 2 * pairs),
            column_from(begin),
            pl.BlockSpec((2, slots, slots), lambda p: (p + begin, 0, 0)),
        ],
        out_specs=[
            column,
            column,
            column,
            pl.BlockSpec((2, 8, 2 * slots), lambda p: (p, 0, 0)),
        ],
        out_shape=[jax.ShapeDtypeStruct((slots, width), LOW)] * 3
        + [jax.ShapeDtypeStruct((2 * count, 8, 2 * slots), FULL)],
        scratch_shapes=[pltpu.VMEM((ROWS, 2 * slots), FULL), pltpu.VMEM((slots, slots), LOW)],
        compiler_params=pltpu.CompilerParams(vmem_limit_bytes=VMEM_BYTES),
        cost_estimate=small_cost(
            flops=2 * count * slots * slots * HEAD_DIM * 32,
            bytes_accessed=2 * count * slots * slots * 2 + 14 * slots * width,
            transcendentals=0,
        ),
        name="attend_back",
    )(projected, projected, projected, grad_attended, probs)


def expert_forward_kernel(rows, first, second, y_out, hidden_out, slope_out, y_sum):
    chunk = pl.program_id(0)
    count = rows.shape[1]
    step = min(256, count)

    @pl.when(chunk == 0)
    def _():
        y_sum[...] = jnp.zeros_like(y_sum)

    for block in range(count // step):
        some = pl.ds(block * step, step)
        pre = mm(rows[0, some, :], first[0], ((1,), (0,)))
        normal_cdf = 0.5 + 0.5 * lax.erf(pre * 0.7071067811865476)
        slope = normal_cdf + pre * jnp.exp(-0.5 * pre * pre) * 0.3989422804014327
        hidden = (pre * normal_cdf).astype(LOW)
        hidden_out[0, some, :] = hidden
        slope_out[0, some, :] = slope.astype(LOW)
        y_sum[some, :] += mm(hidden, second[0], ((1,), (0,)))

    @pl.when(chunk == pl.num_programs(0) - 1)
    def _():
        y_out[...] = y_sum[...].astype(LOW)


def expert_specs(expert, count, width, units):
    def part(*shape):
        return pl.BlockSpec((1,) + shape, lambda c: (c, 0, 0))

    rows_in = pl.BlockSpec((1, count, width), lambda c: (expert, 0, 0))
    rows_out = pl.BlockSpec((count, width), lambda c: (0, 0))
    return (rows_in, rows_out, part(width, units), part(units, width), part(count, units))


def expert_forward(expert, rows, first, second):
    chunks, width, units = first.shape
    count = rows.shape[1]
    rows_in, rows_out, first_spec, second_spec, unit_spec = expert_specs(expert, count, width, units)
    hidden_shape = jax.ShapeDtypeStruct((chunks, count, units), LOW)
    return pl.pallas_call(
        expert_forward_kernel,
        grid=(chunks,),
        in_specs=[rows_in, first_spec, second_spec],
        out_specs=[rows_out, unit_spec, unit_spec],
        out_shape=[jax.ShapeDtypeStruct((count, width), LOW), hidden_shape, hidden_shape],
        scratch_shapes=[pltpu.VMEM((count, width), FULL)],
        compiler_params=pltpu.CompilerParams(vmem_limit_bytes=VMEM_BYTES),
        cost_estimate=small_cost(
            flops=chunks * 4 * count * width * units,
            bytes_accessed=4 * count * width + 4 * chunks * (width + count) * units,
            transcendentals=2 * chunks * count * units,
        ),
        name="expert_forward",
    )(rows, first, second)


def expert_back_kernel(
    rows, grads, first, second, hidden, slope, back_out, first_out, second_out, back_sum, pre_low
):
    chunk = pl.program_id(0)
    count = rows.shape[1]
    step = min(256, count)

    @pl.when(chunk == 0)
    def _():
        back_sum[...] = jnp.zeros_like(back_sum)

    for block in range(count // step):
        some = pl.ds(block * step, step)
        grad_hidden = mm(grads[0, some, :], second[0], ((1,), (1,)))
        grad_pre = (grad_hidden * slope[0, some, :].astype(FULL)).astype(LOW)
        pre_low[some, :] = grad_pre
        back_sum[some, :] += mm(grad_pre, first[0], ((1,), (1,)))
    first_out[0] = mm(rows[0], pre_low[...], ((0,), (0,)), LOW)
    second_out[0] = mm(hidden[0], grads[0], ((0,), (0,)), LOW)

    @pl.when(chunk == pl.num_programs(0) - 1)
    def _():
        back_out[...] = back_sum[...].astype(LOW)


def expert_back(expert, rows, grads, first, second, hidden, slope):
    chunks, width, units = first.shape
    count = rows.shape[1]
    rows_in, rows_out, first_spec, second_spec, unit_spec = expert_specs(expert, count, width, units)
    return pl.pallas_call(
        expert_back_kernel,
        grid=(chunks,),
        in_specs=[rows_in, rows_in, first_spec, second_spec, unit_spec, unit_spec],
        out_specs=[rows_out, first_spec, second_spec],
        out_shape=[
            jax.ShapeDtypeStruct((count, width), LOW),
            jax.ShapeDtypeStruct(first.shape, LOW),
            jax.ShapeDtypeStruct(second.shape, LOW),
        ],
        scratch_shapes=[pltpu.VMEM((count, width), FULL), pltpu.VMEM((count, units), LOW)],
        compiler_params=pltpu.CompilerParams(vmem_limit_bytes=VMEM_BYTES),
        cost_estimate=small_cost(
            flops=chunks * 8 * count * width * units,
            bytes_accessed=6 * count * width + 4 * chunks * (2 * width + count) * units,
            transcendentals=0,
        ),
        name="expert_back",
    )(rows, grads, first, second, hidden, slope)


def place_kernel(groups, hot, *refs):
    *parts, out = refs
    size = len(parts) // groups
    width = parts[0].shape[1]
    for group in range(groups):
        some = [part[...] for part in parts[group * size : (group + 1) * size]]
        values = jnp.concatenate(some, axis=0)
        out[0, :, group * width : (group + 1) * width] = mm(hot[0], values, ((1,), (0,)), LOW)


def place_rows(hot, groups, capacity):
    blocks, count, slots = hot.shape
    parts = sum(groups, [])
    width = parts[0].shape[1]
    wide = width * len(groups)
    return pl.pallas_call(
        partial(place_kernel, len(groups)),
        grid=(blocks,),
        in_specs=[pl.BlockSpec((1, count, slots), lambda b: (b, 0, 0))]
        + [pl.BlockSpec((capacity, width), lambda b: (b, 0))] * len(parts),
        out_specs=pl.BlockSpec((1, count, wide), lambda b: (b, 0, 0)),
        out_shape=jax.ShapeDtypeStruct((blocks, count, wide), LOW),
        compiler_params=pltpu.CompilerParams(vmem_limit_bytes=VMEM_BYTES),
        cost_estimate=small_cost(
            flops=2 * blocks * count * slots * wide,
            bytes_accessed=4 * blocks * count * wide,
            transcendentals=0,
        ),
        name="place_rows",
    )(hot, *parts)


def body(
    tokens,
    cotangent,
    seq_lens,
    routes,
    norm_gains,
    qkv_weight,
    out_weight,
    router_weight,
    rel_bias,
    expert_in,
    expert_out,
):
    tok_count, width = tokens.shape
    bucket_count = rel_bias.shape[0]
    shard_rows = qkv_weight.shape[0]
    experts_all = router_weight.shape[1]
    local_experts = expert_in.shape[0]
    capacity = 2 * tok_count // experts_all
    places = lax.axis_size("fsdp") // 2
    place = lax.axis_index("fsdp") // 2
    peer = lax.axis_index("dp")
    peer_count = lax.axis_size("dp")
    core = ("dp", 1)
    dims = [("fsdp", 1)]
    mask = 2
    while mask < peer_count:
        dims.append(("dp", mask))
        mask *= 2

    spare = -(4 * width + experts_all + 2) % 128
    packed = jnp.concatenate(
        (
            qkv_weight,
            out_weight,
            router_weight,
            norm_gains.T,
            jnp.zeros((shard_rows, spare), LOW),
        ),
        axis=1,
    )
    dense, near = dense_gather(packed, places, place, dims, core)
    qkv_full = dense[:, : 3 * width]
    out_full = dense[:, 3 * width : 4 * width]
    router_full = dense[:, 4 * width : 4 * width + experts_all]
    gains_float = dense[:, 4 * width + experts_all : 4 * width + experts_all + 2].T.astype(FULL)

    groups = z_groups(places)
    weights = []
    for expert in range(local_experts):
        own = (expert_in[expert], expert_out[expert])
        if expert > 0:
            own = after(own, (near,))
        weights.append([lax.all_gather(v, "fsdp", axis=0, axis_index_groups=groups) for v in own])

    chosen = routes[:, 0]
    chosen_hot = chosen[:, None] == jnp.arange(experts_all, dtype=jnp.int32)[None, :]
    order = jnp.arange(tok_count, dtype=jnp.int32)
    earlier = (order[:, None] > order[None, :]).astype(LOW)
    rank_all = jnp.dot(earlier, chosen_hot.astype(LOW), preferred_element_type=FULL)
    rank_in = jnp.sum(jnp.where(chosen_hot, rank_all, 0.0), axis=1).astype(jnp.int32)
    slots_of = gather_blocks((chosen * capacity + rank_in)[None, :], dims)
    keys = sorted(slots_of)
    slots_near = jnp.stack([slots_of[key][0] for key in keys])
    local_slots = local_experts * capacity
    slot_ids = jnp.arange(local_slots, dtype=jnp.int32).reshape(local_experts, capacity)

    def hot_of(owner):
        wanted = owner * local_slots + slot_ids
        return (slots_near[:, None, None, :] == wanted[None, :, :, None]).astype(LOW)

    hot_own, hot_other = hot_of(peer), hot_of(peer ^ 1)
    segment = segment_ids(seq_lens[0], tok_count)
    bucket_hot = diagonal_hot(tok_count, bucket_count)
    base = jnp.einsum("rjb,bh->hrj", bucket_hot, rel_bias, precision=HIGH)

    inputs = tokens.astype(FULL)
    normed_one, inverse_one = rms_parts(inputs, gains_float[0])
    normed_low = normed_one.astype(LOW)
    projected = jnp.dot(normed_low, qkv_full, preferred_element_type=FULL).astype(LOW)
    attended, probs = attend_forward(projected, base, segment[:, None], segment[None, :])
    hidden_one = inputs + jnp.dot(attended, out_full, preferred_element_type=FULL)
    normed_two, inverse_two = rms_parts(hidden_one, gains_float[1])
    normed_two_low = normed_two.astype(LOW)
    router_soft = softmax_rows(jnp.dot(normed_two_low, router_full, preferred_element_type=FULL))
    gate_value = jnp.sum(jnp.where(chosen_hot, router_soft, 0.0), axis=1)
    upstream = cotangent.astype(FULL)
    grad_y = (gate_value[:, None] * upstream).astype(LOW)

    def pick(hot, blocks):
        return jnp.einsum("bjst,btd->jbsd", hot, blocks, preferred_element_type=FULL).astype(LOW)

    def to_rows(blocks):
        other = swap(pick(hot_other, blocks), core)
        both = jnp.stack((pick(hot_own, blocks), other), axis=1)
        return both.reshape(local_experts, -1, width)

    token_ids = jnp.concatenate((peer * local_slots + slot_ids, (peer ^ 1) * local_slots + slot_ids))
    hot_back = (slots_near[:, :, None] == token_ids.reshape(-1)[None, None, :]).astype(LOW)

    def from_rows(*groups):
        near_rows = len(keys) * capacity
        parts = [
            list(values) + [swap(value[near_rows:], core) for value in values] for values in groups
        ]
        return place_rows(hot_back, parts, capacity)

    blocks, brought = gather_halves(normed_two_low, dims)
    rows = to_rows(blocks)
    grad_half = tok_count // 2
    grad_parts = after((grad_y[:grad_half], grad_y[grad_half:]), brought[0])
    held = [{(): part} for part in grad_parts]
    grad_brought = []
    forwards = []
    for number in range(len(dims)):
        steps = (dims[number], dims[len(dims) - 1 - number])
        arrived = [gather_step(part, dim) for part, dim in zip(held, steps)]
        if number == len(dims) - 1:
            (tied,) = after((rows,), sum(grad_brought, []))
            forwards.append(expert_forward(0, tied, *weights[0]))
            arrived = after(arrived, (forwards[0][0],))
        grad_brought.append(arrived)
        held = [gather_join(*of) for of in zip(held, steps, arrived)]
    grad_blocks = jnp.stack(
        [jnp.concatenate((held[0][key], held[1][key])) for key in sorted(held[0])]
    )
    grads = to_rows(grad_blocks)
    backs = []
    for expert in range(local_experts):
        if expert > 0:
            (tied,) = after((rows,), (backs[-1][0],))
            forwards.append(expert_forward(expert, tied, *weights[expert]))
        backs.append(expert_back(expert, rows, grads, *weights[expert], *forwards[expert][1:]))
    summed = [
        [
            lax.psum_scatter(
                value, "fsdp", scatter_dimension=0, axis_index_groups=groups, tiled=False
            )
            for value in back[1:]
        ]
        for back in backs
    ]
    returned = scatter_halves(
        from_rows([forward[0] for forward in forwards], [back[0] for back in backs]), keys, dims
    )
    token_y, grad_rows = returned[:, :width], returned[:, width:]

    mixed = (hidden_one + gate_value[:, None] * token_y).astype(LOW)
    grad_gate = jnp.sum(upstream * token_y, axis=1)
    grad_logits = router_soft * (
        jnp.where(chosen_hot, grad_gate[:, None], 0.0) - (gate_value * grad_gate)[:, None]
    )
    router_local = jnp.dot(normed_two_low.astype(FULL).T, grad_logits, precision=HIGH)
    grad_normed_two = grad_rows + jnp.dot(
        grad_logits, router_full.astype(FULL).T, precision=HIGH
    )
    grad_from_two, gain_grad_two = norm_back(
        hidden_one, inverse_two, gains_float[1], grad_normed_two
    )
    grad_hidden_one = upstream + grad_from_two
    grad_attn_low = grad_hidden_one.astype(LOW)
    out_local = jnp.einsum("td,te->de", attended, grad_attn_low, preferred_element_type=FULL)
    grad_attended = mm(grad_attn_low, out_full, ((1,), (1,)), LOW)
    names = ["z", dims[0]] + sorted(dims[1:], reverse=True) + [core]

    def split_rows(panel):
        shape = (places,) + (2,) * (len(names) - 1) + (shard_rows, panel.shape[1])
        parts, left, _ = halve([panel.reshape(shape)], [names], [core])
        return (parts[0], left[0])

    spare_out = -(experts_all + 2) % 128
    out_panel = jnp.concatenate(
        (
            out_local.astype(LOW),
            router_local.astype(LOW),
            gain_grad_two[:, None].astype(LOW),
            jnp.zeros((width, spare_out + 1), LOW),
        ),
        axis=1,
    )
    out_half, half_names = split_rows(out_panel)
    early = [value for back in summed[:-1] for value in back]
    (grad_attended,) = after((grad_attended,), early)
    *grad_parts, diagonals = attend_back(projected, grad_attended, probs, 0, HEADS // 2)
    grad_projected = jnp.concatenate(grad_parts, axis=1)
    qkv_local = mm(normed_low, grad_projected, ((0,), (0,)), LOW)
    qkv_half, _ = split_rows(qkv_local)
    half = 3 * width // 2
    grad_normed_one = mm(grad_projected, qkv_full, ((1,), (1,)))
    grad_from_one, gain_grad_one = norm_back(inputs, inverse_one, gains_float[0], grad_normed_one)
    tokens_grad = grad_hidden_one + grad_from_one
    bias_local = jnp.einsum("hrj,rjb->bh", diagonals, bucket_hot, precision=HIGH)
    gain_rows = width // 128
    small = jnp.concatenate((bias_local.reshape(-1, 128), gain_grad_one.reshape(-1, 128)))
    (first_sum, second_sum, out_sum), small = dense_scatter(
        [qkv_half[..., :half], qkv_half[..., half:], out_half],
        half_names,
        [dims, dims[::-1], dims[::-1]],
        places,
        place,
        small,
        [core] + dims,
    )
    summed[-1] = after(summed[-1], (first_sum, second_sum))
    in_grad, out_expert_grad = (
        jnp.stack([back[which].astype(FULL) for back in summed]) for which in (0, 1)
    )
    qkv_grad = jnp.concatenate((first_sum, second_sum), axis=1)
    bias_grad = small[:-gain_rows].reshape(bias_local.shape)
    device = lax.axis_index("fsdp") * peer_count + peer
    gain_one = lax.dynamic_slice_in_dim(
        small[-gain_rows:].reshape(-1), device * shard_rows, shard_rows
    )
    gains_grad = jnp.stack((gain_one, out_sum[:, width + experts_all]))
    router_grad = out_sum[:, width : width + experts_all]
    out_grad = out_sum[:, :width]
    return (
        mixed,
        tokens_grad,
        gains_grad,
        qkv_grad,
        out_grad,
        router_grad,
        bias_grad,
        in_grad,
        out_expert_grad,
    )


def solution(mesh):
    rows = P(("fsdp", "dp"), None)
    columns = P(None, ("fsdp", "dp"))
    experts = (P("dp", None, "fsdp"), P("dp", "fsdp", None))
    return jax.shard_map(
        body,
        mesh=mesh,
        in_specs=(rows, rows, rows, rows, columns, rows, rows, rows, P()) + experts,
        out_specs=(rows, rows, columns, rows, rows, rows, P()) + experts,
        check_vma=False,
    )
```

```python
from functools import partial, reduce

import jax
import jax.numpy as jnp
from jax import lax
from jax.experimental import pallas as pl
from jax.experimental.pallas import tpu as pltpu
from jax.sharding import PartitionSpec as P

HEADS = 12
HEAD_DIM = 64
EPS = 1e-06
LIMITS = (12, 16, 23, 32, 46, 64, 91)
SCALE = 0.125
HIGH = lax.Precision.HIGHEST
LOW = jnp.bfloat16
FULL = jnp.float32
ROWS = 128
VMEM_BYTES = 52 * 1024 * 1024


def bucket_index(relative):
    distance = jnp.abs(relative)
    far_bucket = reduce(
        lambda counted, boundary: counted + (distance >= boundary).astype(jnp.int32),
        LIMITS,
        jnp.full_like(distance, 8),
    )
    return jnp.where(distance < 8, distance, far_bucket) + 16 * (relative > 0).astype(jnp.int32)


def segment_ids(lengths, slots):
    ending = jnp.cumsum(lengths)
    places = jnp.arange(slots, dtype=jnp.int32)
    return jnp.sum((places[:, None] >= ending[None, :]).astype(jnp.int32), axis=1)


def rms_parts(values, gain):
    inverse = lax.rsqrt(jnp.mean(values * values, axis=-1, keepdims=True) + EPS)
    return (values * inverse * gain, inverse)


def norm_back(values, inverse, gain, upstream):
    scaled = upstream * gain
    grad_values = inverse * scaled - values * inverse * inverse * inverse * jnp.mean(
        values * scaled, axis=-1, keepdims=True
    )
    return (grad_values, jnp.sum(upstream * values * inverse, axis=0))


def softmax_rows(scores):
    highest = jnp.max(scores, axis=-1, keepdims=True)
    raised = jnp.exp(scores - highest)
    return raised / jnp.sum(raised, axis=-1, keepdims=True)


def mm(left, right, contract, out=FULL):
    return lax.dot_general(left, right, (contract, ((), ())), preferred_element_type=FULL).astype(
        out
    )


def small_cost(flops, bytes_accessed, transcendentals):
    return pl.CostEstimate(
        flops=flops // 64,
        bytes_accessed=bytes_accessed // 64,
        transcendentals=transcendentals // 64,
    )


def nothing_kernel(*refs):
    del refs


def after(values, deps):
    values, deps = list(values), list(deps)
    anywhere = pl.BlockSpec(memory_space=pl.ANY)
    return pl.pallas_call(
        nothing_kernel,
        in_specs=[anywhere] * (len(values) + len(deps)),
        out_specs=[anywhere] * len(values),
        out_shape=[jax.ShapeDtypeStruct(value.shape, value.dtype) for value in values],
        input_output_aliases={number: number for number in range(len(values))},
        name="after",
    )(*values, *deps)


def swap(value, dim):
    axis, mask = dim
    count = lax.axis_size(axis)
    return lax.ppermute(value, axis, [(i, i ^ mask) for i in range(count)])


def bit_of(dim):
    axis, mask = dim
    return (lax.axis_index(axis) & mask) != 0


def stage_pair(value, dim):
    other = swap(value, dim)
    return jnp.where(bit_of(dim), jnp.stack((other, value)), jnp.stack((value, other)))


def ring_shift(value, places, by):
    count = 2 * places
    return lax.ppermute(value, "fsdp", [(i, (i - 2 * by) % count) for i in range(count)])


def z_gather(value, places, place):
    parts = jnp.stack([value] + [ring_shift(value, places, by) for by in range(1, places)])
    return lax.dynamic_slice_in_dim(
        jnp.concatenate((parts, parts)), lax.rem(places - place, places), places, 0
    )


def z_groups(places):
    return [[2 * place + side for place in range(places)] for side in (0, 1)]


def gather_step(held, dim):
    keys = list(held)
    value = jnp.stack([held[key] for key in keys]) if len(keys) > 1 else held[keys[0]]
    return swap(value, dim)


def gather_join(held, dim, arrived):
    keys = list(held)
    joined = dict(held)
    for number, key in enumerate(keys):
        joined[tuple(sorted(key + (dim,)))] = arrived[number] if len(keys) > 1 else arrived
    return joined


def gather_blocks(value, dims):
    held = {(): value}
    for dim in dims:
        held = gather_join(held, dim, gather_step(held, dim))
    return held


def gather_halves(value, dims):
    half = value.shape[0] // 2
    held = [{(): value[:half]}, {(): value[half:]}]
    brought = []
    for number in range(len(dims)):
        steps = (dims[number], dims[len(dims) - 1 - number])
        arrived = after([gather_step(part, dim) for part, dim in zip(held, steps)], ())
        brought.append(arrived)
        held = [gather_join(*of) for of in zip(held, steps, arrived)]
    upper, lower = held
    blocks = jnp.stack([jnp.concatenate((upper[key], lower[key])) for key in sorted(upper)])
    return (blocks, brought)


def scatter_halves(blocks, keys, dims):
    half = blocks.shape[1] // 2
    parts = [
        {key: blocks[number, :half] for number, key in enumerate(keys)},
        {key: blocks[number, half:] for number, key in enumerate(keys)},
    ]
    for number in range(len(dims)):
        steps = (dims[len(dims) - 1 - number], dims[number])
        stay = [[key for key in held if dim not in key] for held, dim in zip(parts, steps)]
        sent = [
            jnp.stack([held[tuple(sorted(key + (dim,)))].astype(LOW) for key in some])
            for held, dim, some in zip(parts, steps, stay)
        ]
        arrived = after([swap(value, dim) for value, dim in zip(sent, steps)], ())
        parts = [
            {
                key: held[key].astype(FULL) + value[place].astype(FULL)
                for place, key in enumerate(some)
            }
            for held, value, some in zip(parts, arrived, stay)
        ]
    return jnp.concatenate((parts[0][()], parts[1][()]))


def dense_gather(value, places, place, dims, core):
    columns = value.shape[1]
    half = (columns // 256) * 128
    near = z_gather(value, places, place)
    wanted = ("z", dims[0]) + tuple(sorted(dims[1:], reverse=True)) + ("core", "rows", "columns")

    def run(part, order):
        axes = ("z", "rows", "columns")
        for dim in order:
            part = stage_pair(part, dim)
            axes = (dim,) + axes
        part = stage_pair(part, core)
        axes = ("core",) + axes
        return part.transpose([axes.index(name) for name in wanted]).reshape(-1, part.shape[-1])

    first = run(near[..., :half], dims)
    second = run(near[..., half:], list(reversed(dims)))
    return (jnp.concatenate((first, second), axis=1), near)


def halve(parts, all_names, dims, beside=()):
    kept, sent, left = [], [], []
    for part, names, dim in zip(parts, all_names, dims):
        spot = names.index(dim)
        own = bit_of(dim).astype(jnp.int32)
        kept.append(lax.dynamic_index_in_dim(part, own, spot, keepdims=False))
        send = lax.dynamic_index_in_dim(part, 1 - own, spot, keepdims=False)
        sent.append(swap(send, dim))
        left.append(names[:spot] + names[spot + 1 :])
    arrived = after(sent + list(beside), ())
    sums = [(a.astype(FULL) + b.astype(FULL)).astype(LOW) for a, b in zip(kept, arrived)]
    return (sums, left, arrived[len(sent) :])


def add_up(value, others):
    return reduce(lambda total, other: total + other, others, value)


def dense_scatter(parts, names, orders, groups, small):
    all_names = [names] * len(parts)
    places = len(groups[0])
    for number, dims in enumerate(zip(*orders)):
        beside = ()
        if number == 0:
            beside = [swap(small, ("dp", mask)) for mask in range(1, lax.axis_size("dp"))]
        elif number == 1:
            beside = [swap(small, ("fsdp", 1))]
        parts, all_names, others = halve(parts, all_names, dims, beside)
        small = add_up(small, others)
    joined = jnp.concatenate(parts, axis=-1)
    moved = lax.all_to_all(
        joined, "fsdp", split_axis=0, concat_axis=0, axis_index_groups=groups, tiled=True
    )
    near = [ring_shift(small, places, by) for by in range(1, places)]
    moved, *others = after([moved] + near, ())
    return (jnp.sum(moved.astype(FULL), axis=0), add_up(small, others))


def diagonal_hot(slots, bucket_count):
    width = 2 * slots
    lanes = jnp.arange(width, dtype=jnp.int32)[None, :]
    rows = jnp.arange(8, dtype=jnp.int32)[:, None]
    diagonal = (lanes - rows + (ROWS - 1)) % width
    bucket = jnp.where(diagonal < width - 1, bucket_index(diagonal - (slots - 1)), -1)
    return (bucket[:, :, None] == jnp.arange(bucket_count, dtype=jnp.int32)).astype(FULL)


def attend_kernel(query, key, value, base, seg_col, seg_row, out, probs, toeplitz):
    slots = query.shape[0]
    lanes = lax.broadcasted_iota(jnp.int32, (1, 2 * HEAD_DIM), 1)
    total = [None] * (slots // ROWS)
    for head in range(2):
        mine = (lanes >= head * HEAD_DIM) & (lanes < (head + 1) * HEAD_DIM)
        table = base[head]
        size = 8
        while size < ROWS:
            table = jnp.concatenate((table, pltpu.roll(table, size, 1)), axis=0)
            size *= 2
        toeplitz[...] = table
        value_head = jnp.where(mine, value[...], 0).astype(LOW)
        for block in range(slots // ROWS):
            rows = pl.ds(block * ROWS, ROWS)
            query_head = jnp.where(mine, query[rows, :], 0).astype(LOW)
            shift = slots - ROWS - block * ROWS
            scores = mm(query_head, key[...], ((1,), (1,))) * SCALE
            scores = scores + toeplitz[:, shift : shift + slots]
            scores = jnp.where(seg_col[rows, :] == seg_row[...], scores, -1e30)
            highest = jnp.max(scores, axis=-1, keepdims=True)
            raised = jnp.exp(scores - highest)
            low = (raised / jnp.sum(raised, axis=-1, keepdims=True)).astype(LOW)
            probs[head, rows, :] = low
            part = mm(low, value_head, ((1,), (0,)))
            total[block] = part if head == 0 else total[block] + part
    for block in range(slots // ROWS):
        out[pl.ds(block * ROWS, ROWS), :] = total[block].astype(LOW)


def attend_forward(projected, base, seg_col, seg_row):
    slots = projected.shape[0]
    width = projected.shape[1] // 3
    pairs = HEADS // 2
    lanes = 2 * HEAD_DIM
    return pl.pallas_call(
        attend_kernel,
        grid=(pairs,),
        in_specs=[
            pl.BlockSpec((slots, lanes), lambda p: (0, p)),
            pl.BlockSpec((slots, lanes), lambda p: (0, p + pairs)),
            pl.BlockSpec((slots, lanes), lambda p: (0, p + 2 * pairs)),
            pl.BlockSpec((2, 8, 2 * slots), lambda p: (p, 0, 0)),
            pl.BlockSpec((slots, 1), lambda p: (0, 0)),
            pl.BlockSpec((1, slots), lambda p: (0, 0)),
        ],
        out_specs=[
            pl.BlockSpec((slots, lanes), lambda p: (0, p)),
            pl.BlockSpec((2, slots, slots), lambda p: (p, 0, 0)),
        ],
        out_shape=[
            jax.ShapeDtypeStruct((slots, width), LOW),
            jax.ShapeDtypeStruct((HEADS, slots, slots), LOW),
        ],
        scratch_shapes=[pltpu.VMEM((ROWS, 2 * slots), FULL)],
        compiler_params=pltpu.CompilerParams(vmem_limit_bytes=VMEM_BYTES),
        cost_estimate=small_cost(
            flops=HEADS * slots * slots * HEAD_DIM * 16,
            bytes_accessed=HEADS * slots * slots * 2 + 8 * slots * width,
            transcendentals=HEADS * slots * slots,
        ),
        name="attend_forward",
    )(projected, projected, projected, base, seg_col, seg_row)


def attend_back_kernel(
    query, key, value, grad, probs, out_query, out_key, out_value, diagonals, lined, scores_low
):
    slots = query.shape[0]
    lanes = lax.broadcasted_iota(jnp.int32, (1, 2 * HEAD_DIM), 1)
    query_total = [None] * (slots // ROWS)
    key_total = value_total = None
    for head in range(2):
        mine = (lanes >= head * HEAD_DIM) & (lanes < (head + 1) * HEAD_DIM)
        key_head = jnp.where(mine, key[...], 0).astype(LOW)
        grad_head = jnp.where(mine, grad[...], 0).astype(LOW)
        query_head = jnp.where(mine, query[...], 0).astype(LOW)
        lined[...] = jnp.zeros_like(lined)
        for block in range(slots // ROWS):
            rows = pl.ds(block * ROWS, ROWS)
            soft = probs[head, rows, :].astype(FULL)
            grad_rows = jnp.where(mine, grad[rows, :], 0).astype(LOW)
            weighted = soft * mm(grad_rows, value[...], ((1,), (1,)))
            back = weighted - soft * jnp.sum(weighted, axis=-1, keepdims=True)
            low = back.astype(LOW)
            scores_low[rows, :] = low
            shift = slots - ROWS - block * ROWS
            lined[:, shift : shift + slots] += low.astype(FULL)
            part = mm(low, key_head, ((1,), (0,)))
            query_total[block] = part if head == 0 else query_total[block] + part
        key_part = mm(scores_low[...], query_head, ((0,), (0,)))
        value_part = mm(probs[head], grad_head, ((0,), (0,)))
        key_total = key_part if head == 0 else key_total + key_part
        value_total = value_part if head == 0 else value_total + value_part
        table = lined[...]
        size = ROWS
        while size > 8:
            size //= 2
            table = table[:size] + pltpu.roll(table[size:], 2 * slots - size, 1)
        diagonals[head] = table
    out_key[...] = (key_total * SCALE).astype(LOW)
    out_value[...] = value_total.astype(LOW)
    for block in range(slots // ROWS):
        out_query[pl.ds(block * ROWS, ROWS), :] = (query_total[block] * SCALE).astype(LOW)


def attend_back(projected, grad_attended, probs, begin, count):
    slots = projected.shape[0]
    pairs = HEADS // 2
    lanes = 2 * HEAD_DIM
    width = count * lanes
    column = pl.BlockSpec((slots, lanes), lambda p: (0, p))

    def column_from(offset):
        return pl.BlockSpec((slots, lanes), lambda p: (0, p + offset))

    return pl.pallas_call(
        attend_back_kernel,
        grid=(count,),
        in_specs=[
            column_from(begin),
            column_from(begin + pairs),
            column_from(begin + 2 * pairs),
            column_from(begin),
            pl.BlockSpec((2, slots, slots), lambda p: (p + begin, 0, 0)),
        ],
        out_specs=[
            column,
            column,
            column,
            pl.BlockSpec((2, 8, 2 * slots), lambda p: (p, 0, 0)),
        ],
        out_shape=[jax.ShapeDtypeStruct((slots, width), LOW)] * 3
        + [jax.ShapeDtypeStruct((2 * count, 8, 2 * slots), FULL)],
        scratch_shapes=[pltpu.VMEM((ROWS, 2 * slots), FULL), pltpu.VMEM((slots, slots), LOW)],
        compiler_params=pltpu.CompilerParams(vmem_limit_bytes=VMEM_BYTES),
        cost_estimate=small_cost(
            flops=2 * count * slots * slots * HEAD_DIM * 32,
            bytes_accessed=2 * count * slots * slots * 2 + 14 * slots * width,
            transcendentals=0,
        ),
        name="attend_back",
    )(projected, projected, projected, grad_attended, probs)


def second_of(weights):
    _, rows, units = weights.shape
    width = rows // 2
    runs = [weights[0, row : row + units, :] for row in range(width, rows, units)]
    return jnp.concatenate(runs, axis=1)


def expert_forward_kernel(rows, weights, y_out, hidden_out, slope_out, y_sum):
    chunk = pl.program_id(0)
    count, width = rows.shape[1:]
    step = min(256, count)
    second = second_of(weights)

    @pl.when(chunk == 0)
    def _():
        y_sum[...] = jnp.zeros_like(y_sum)

    for block in range(count // step):
        some = pl.ds(block * step, step)
        pre = mm(rows[0, some, :], weights[0, :width, :], ((1,), (0,)))
        normal_cdf = 0.5 + 0.5 * lax.erf(pre * 0.7071067811865476)
        slope = normal_cdf + pre * jnp.exp(-0.5 * pre * pre) * 0.3989422804014327
        hidden = (pre * normal_cdf).astype(LOW)
        hidden_out[0, some, :] = hidden
        slope_out[0, some, :] = slope.astype(LOW)
        y_sum[some, :] += mm(hidden, second, ((1,), (0,)))

    @pl.when(chunk == pl.num_programs(0) - 1)
    def _():
        y_out[...] = y_sum[...].astype(LOW)


def expert_specs(expert, count, width, units):
    def part(*shape):
        return pl.BlockSpec((1,) + shape, lambda c: (c, 0, 0))

    rows_in = pl.BlockSpec((1, count, width), lambda c: (expert, 0, 0))
    rows_out = pl.BlockSpec((count, width), lambda c: (0, 0))
    return (rows_in, rows_out, part(2 * width, units), part(count, units))


def expert_forward(expert, rows, weights):
    chunks, _, units = weights.shape
    count, width = rows.shape[1:]
    rows_in, rows_out, weight_spec, unit_spec = expert_specs(expert, count, width, units)
    hidden_shape = jax.ShapeDtypeStruct((chunks, count, units), LOW)
    return pl.pallas_call(
        expert_forward_kernel,
        grid=(chunks,),
        in_specs=[rows_in, weight_spec],
        out_specs=[rows_out, unit_spec, unit_spec],
        out_shape=[jax.ShapeDtypeStruct((count, width), LOW), hidden_shape, hidden_shape],
        scratch_shapes=[pltpu.VMEM((count, width), FULL)],
        compiler_params=pltpu.CompilerParams(vmem_limit_bytes=VMEM_BYTES),
        cost_estimate=small_cost(
            flops=chunks * 4 * count * width * units,
            bytes_accessed=4 * count * width + 4 * chunks * (width + count) * units,
            transcendentals=2 * chunks * count * units,
        ),
        name="expert_forward",
    )(rows, weights)


def expert_back_kernel(
    rows, grads, weights, hidden, slope, back_out, weights_out, back_sum, pre_low
):
    chunk = pl.program_id(0)
    count, width = rows.shape[1:]
    units = weights.shape[2]
    step = min(256, count)
    second = second_of(weights)

    @pl.when(chunk == 0)
    def _():
        back_sum[...] = jnp.zeros_like(back_sum)

    for block in range(count // step):
        some = pl.ds(block * step, step)
        grad_hidden = mm(grads[0, some, :], second, ((1,), (1,)))
        grad_pre = (grad_hidden * slope[0, some, :].astype(FULL)).astype(LOW)
        pre_low[some, :] = grad_pre
        back_sum[some, :] += mm(grad_pre, weights[0, :width, :], ((1,), (1,)))
    weights_out[0, :width, :] = mm(rows[0], pre_low[...], ((0,), (0,)), LOW)
    second_grad = mm(hidden[0], grads[0], ((0,), (0,)), LOW)
    for column in range(0, width, units):
        weights_out[0, width + column : width + column + units, :] = second_grad[
            :, column : column + units
        ]

    @pl.when(chunk == pl.num_programs(0) - 1)
    def _():
        back_out[...] = back_sum[...].astype(LOW)


def expert_back(expert, rows, grads, weights, hidden, slope):
    chunks, _, units = weights.shape
    count, width = rows.shape[1:]
    rows_in, rows_out, weight_spec, unit_spec = expert_specs(expert, count, width, units)
    return pl.pallas_call(
        expert_back_kernel,
        grid=(chunks,),
        in_specs=[rows_in, rows_in, weight_spec, unit_spec, unit_spec],
        out_specs=[rows_out, weight_spec],
        out_shape=[
            jax.ShapeDtypeStruct((count, width), LOW),
            jax.ShapeDtypeStruct(weights.shape, LOW),
        ],
        scratch_shapes=[pltpu.VMEM((count, width), FULL), pltpu.VMEM((count, units), LOW)],
        compiler_params=pltpu.CompilerParams(vmem_limit_bytes=VMEM_BYTES),
        cost_estimate=small_cost(
            flops=chunks * 8 * count * width * units,
            bytes_accessed=6 * count * width + 4 * chunks * (2 * width + count) * units,
            transcendentals=0,
        ),
        name="expert_back",
    )(rows, grads, weights, hidden, slope)


def place_kernel(groups, hot, *refs):
    *parts, out = refs
    size = len(parts) // groups
    width = parts[0].shape[1]
    for group in range(groups):
        some = [part[...] for part in parts[group * size : (group + 1) * size]]
        values = jnp.concatenate(some, axis=0)
        out[0, :, group * width : (group + 1) * width] = mm(hot[0], values, ((1,), (0,)), LOW)


def place_rows(hot, groups, capacity):
    blocks, count, slots = hot.shape
    parts = sum(groups, [])
    width = parts[0].shape[1]
    wide = width * len(groups)
    return pl.pallas_call(
        partial(place_kernel, len(groups)),
        grid=(blocks,),
        in_specs=[pl.BlockSpec((1, count, slots), lambda b: (b, 0, 0))]
        + [pl.BlockSpec((capacity, width), lambda b: (b, 0))] * len(parts),
        out_specs=pl.BlockSpec((1, count, wide), lambda b: (b, 0, 0)),
        out_shape=jax.ShapeDtypeStruct((blocks, count, wide), LOW),
        compiler_params=pltpu.CompilerParams(vmem_limit_bytes=VMEM_BYTES),
        cost_estimate=small_cost(
            flops=2 * blocks * count * slots * wide,
            bytes_accessed=4 * blocks * count * wide,
            transcendentals=0,
        ),
        name="place_rows",
    )(hot, *parts)


def body(
    tokens,
    cotangent,
    seq_lens,
    routes,
    norm_gains,
    qkv_weight,
    out_weight,
    router_weight,
    rel_bias,
    expert_in,
    expert_out,
):
    tok_count, width = tokens.shape
    bucket_count = rel_bias.shape[0]
    shard_rows = qkv_weight.shape[0]
    experts_all = router_weight.shape[1]
    local_experts, _, units = expert_in.shape
    capacity = 2 * tok_count // experts_all
    places = lax.axis_size("fsdp") // 2
    place = lax.axis_index("fsdp") // 2
    peer = lax.axis_index("dp")
    peer_count = lax.axis_size("dp")
    core = ("dp", 1)
    dims = [("fsdp", 1)]
    mask = 2
    while mask < peer_count:
        dims.append(("dp", mask))
        mask *= 2

    spare = -(4 * width + experts_all + 2) % 128
    packed = jnp.concatenate(
        (
            qkv_weight,
            out_weight,
            router_weight,
            norm_gains.T,
            jnp.zeros((shard_rows, spare), LOW),
        ),
        axis=1,
    )
    dense, near = dense_gather(packed, places, place, dims, core)
    qkv_full = dense[:, : 3 * width]
    out_full = dense[:, 3 * width : 4 * width]
    router_full = dense[:, 4 * width : 4 * width + experts_all]
    gains_float = dense[:, 4 * width + experts_all : 4 * width + experts_all + 2].T.astype(FULL)

    groups = z_groups(places)
    weights = []
    for expert in range(local_experts):
        runs = [expert_out[expert][:, row : row + units] for row in range(0, width, units)]
        own = jnp.concatenate([expert_in[expert]] + runs)
        if expert > 0:
            (own,) = after((own,), (near,))
        weights.append(lax.all_gather(own, "fsdp", axis=0, axis_index_groups=groups))

    chosen = routes[:, 0]
    chosen_hot = chosen[:, None] == jnp.arange(experts_all, dtype=jnp.int32)[None, :]
    order = jnp.arange(tok_count, dtype=jnp.int32)
    earlier = (order[:, None] > order[None, :]).astype(LOW)
    rank_all = jnp.dot(earlier, chosen_hot.astype(LOW), preferred_element_type=FULL)
    rank_in = jnp.sum(jnp.where(chosen_hot, rank_all, 0.0), axis=1).astype(jnp.int32)
    slots_of = gather_blocks((chosen * capacity + rank_in)[None, :], dims)
    keys = sorted(slots_of)
    slots_near = jnp.stack([slots_of[key][0] for key in keys])
    local_slots = local_experts * capacity
    slot_ids = jnp.arange(local_slots, dtype=jnp.int32).reshape(local_experts, capacity)

    def hot_of(owner):
        wanted = owner * local_slots + slot_ids
        return (slots_near[:, None, None, :] == wanted[None, :, :, None]).astype(LOW)

    hot_own, hot_other = hot_of(peer), hot_of(peer ^ 1)
    segment = segment_ids(seq_lens[0], tok_count)
    bucket_hot = diagonal_hot(tok_count, bucket_count)
    base = jnp.einsum("rjb,bh->hrj", bucket_hot, rel_bias, precision=HIGH)

    inputs = tokens.astype(FULL)
    normed_one, inverse_one = rms_parts(inputs, gains_float[0])
    normed_low = normed_one.astype(LOW)
    projected = jnp.dot(normed_low, qkv_full, preferred_element_type=FULL).astype(LOW)
    attended, probs = attend_forward(projected, base, segment[:, None], segment[None, :])
    hidden_one = inputs + jnp.dot(attended, out_full, preferred_element_type=FULL)
    normed_two, inverse_two = rms_parts(hidden_one, gains_float[1])
    normed_two_low = normed_two.astype(LOW)
    router_soft = softmax_rows(jnp.dot(normed_two_low, router_full, preferred_element_type=FULL))
    gate_value = jnp.sum(jnp.where(chosen_hot, router_soft, 0.0), axis=1)
    upstream = cotangent.astype(FULL)
    grad_y = (gate_value[:, None] * upstream).astype(LOW)

    def pick(hot, blocks):
        return jnp.einsum("bjst,btd->jbsd", hot, blocks, preferred_element_type=FULL).astype(LOW)

    def to_rows(blocks):
        other = swap(pick(hot_other, blocks), core)
        both = jnp.stack((pick(hot_own, blocks), other), axis=1)
        return both.reshape(local_experts, -1, width)

    token_ids = jnp.concatenate((peer * local_slots + slot_ids, (peer ^ 1) * local_slots + slot_ids))
    hot_back = (slots_near[:, :, None] == token_ids.reshape(-1)[None, None, :]).astype(LOW)

    def from_rows(*groups):
        near_rows = len(keys) * capacity
        parts = [
            list(values) + [swap(value[near_rows:], core) for value in values] for values in groups
        ]
        return place_rows(hot_back, parts, capacity)

    blocks, brought = gather_halves(normed_two_low, dims)
    rows = to_rows(blocks)
    grad_half = tok_count // 2
    grad_parts = after((grad_y[:grad_half], grad_y[grad_half:]), brought[0])
    held = [{(): part} for part in grad_parts]
    grad_brought = []
    forwards = []
    for number in range(len(dims)):
        steps = (dims[number], dims[len(dims) - 1 - number])
        arrived = [gather_step(part, dim) for part, dim in zip(held, steps)]
        if number == len(dims) - 1:
            (tied,) = after((rows,), sum(grad_brought, []))
            forwards.append(expert_forward(0, tied, weights[0]))
            arrived = after(arrived, (forwards[0][0],))
        grad_brought.append(arrived)
        held = [gather_join(*of) for of in zip(held, steps, arrived)]
    grad_blocks = jnp.stack(
        [jnp.concatenate((held[0][key], held[1][key])) for key in sorted(held[0])]
    )
    grads = to_rows(grad_blocks)
    backs = []
    for expert in range(local_experts):
        if expert > 0:
            (tied,) = after((rows,), (backs[-1][0], hot_back))
            forwards.append(expert_forward(expert, tied, weights[expert]))
        backs.append(expert_back(expert, rows, grads, weights[expert], *forwards[expert][1:]))
    summed = [
        lax.psum_scatter(
            back[1], "fsdp", scatter_dimension=0, axis_index_groups=groups, tiled=False
        )
        for back in backs
    ]
    returned = scatter_halves(
        from_rows([forward[0] for forward in forwards], [back[0] for back in backs]), keys, dims
    )
    token_y, grad_rows = returned[:, :width], returned[:, width:]

    mixed = (hidden_one + gate_value[:, None] * token_y).astype(LOW)
    grad_gate = jnp.sum(upstream * token_y, axis=1)
    grad_logits = router_soft * (
        jnp.where(chosen_hot, grad_gate[:, None], 0.0) - (gate_value * grad_gate)[:, None]
    )
    router_local = jnp.dot(normed_two_low.astype(FULL).T, grad_logits, precision=HIGH)
    grad_normed_two = grad_rows + jnp.dot(
        grad_logits, router_full.astype(FULL).T, precision=HIGH
    )
    grad_from_two, gain_grad_two = norm_back(
        hidden_one, inverse_two, gains_float[1], grad_normed_two
    )
    grad_hidden_one = upstream + grad_from_two
    grad_attn_low = grad_hidden_one.astype(LOW)
    out_local = jnp.einsum("td,te->de", attended, grad_attn_low, preferred_element_type=FULL)
    grad_attended = mm(grad_attn_low, out_full, ((1,), (1,)), LOW)
    names = ["z", dims[0]] + sorted(dims[1:], reverse=True) + [core]

    def split_rows(panel):
        shape = (places,) + (2,) * (len(names) - 1) + (shard_rows, panel.shape[1])
        parts, left, _ = halve([panel.reshape(shape)], [names], [core])
        return (parts[0], left[0])

    spare_out = -(experts_all + 2) % 128
    out_panel = jnp.concatenate(
        (
            out_local.astype(LOW),
            router_local.astype(LOW),
            gain_grad_two[:, None].astype(LOW),
            jnp.zeros((width, spare_out + 1), LOW),
        ),
        axis=1,
    )
    out_half, half_names = split_rows(out_panel)
    early = summed[:-1]
    (grad_attended,) = after((grad_attended,), early)
    *grad_parts, diagonals = attend_back(projected, grad_attended, probs, 0, HEADS // 2)
    grad_projected = jnp.concatenate(grad_parts, axis=1)
    qkv_local = mm(normed_low, grad_projected, ((0,), (0,)), LOW)
    qkv_half, _ = split_rows(qkv_local)
    half = 3 * width // 2
    grad_normed_one = mm(grad_projected, qkv_full, ((1,), (1,)))
    grad_from_one, gain_grad_one = norm_back(inputs, inverse_one, gains_float[0], grad_normed_one)
    tokens_grad = grad_hidden_one + grad_from_one
    bias_local = jnp.einsum("hrj,rjb->bh", diagonals, bucket_hot, precision=HIGH)
    gain_rows = width // 128
    small = jnp.concatenate((bias_local.reshape(-1, 128), gain_grad_one.reshape(-1, 128)))
    dense_sum, small = dense_scatter(
        [qkv_half[..., :half], qkv_half[..., half:], out_half],
        half_names,
        [dims, dims[::-1], dims[::-1]],
        groups,
        small,
    )
    summed[-1:] = after(summed[-1:], (dense_sum,))
    in_grad = jnp.stack([both[:width].astype(FULL) for both in summed])
    out_expert_grad = jnp.stack(
        [
            jnp.concatenate(
                [both[row : row + units].astype(FULL) for row in range(width, 2 * width, units)],
                axis=1,
            )
            for both in summed
        ]
    )
    qkv_grad, out_sum = dense_sum[:, : 3 * width], dense_sum[:, 3 * width :]
    bias_grad = small[:-gain_rows].reshape(bias_local.shape)
    device = lax.axis_index("fsdp") * peer_count + peer
    gain_one = lax.dynamic_slice_in_dim(
        small[-gain_rows:].reshape(-1), device * shard_rows, shard_rows
    )
    gains_grad = jnp.stack((gain_one, out_sum[:, width + experts_all]))
    router_grad = out_sum[:, width : width + experts_all]
    out_grad = out_sum[:, :width]
    return (
        mixed,
        tokens_grad,
        gains_grad,
        qkv_grad,
        out_grad,
        router_grad,
        bias_grad,
        in_grad,
        out_expert_grad,
    )


def solution(mesh):
    rows = P(("fsdp", "dp"), None)
    columns = P(None, ("fsdp", "dp"))
    experts = (P("dp", None, "fsdp"), P("dp", "fsdp", None))
    return jax.shard_map(
        body,
        mesh=mesh,
        in_specs=(rows, rows, rows, rows, columns, rows, rows, rows, P()) + experts,
        out_specs=(rows, rows, columns, rows, rows, rows, P()) + experts,
        check_vma=False,
    )
```

```python
from functools import partial, reduce

import jax
import jax.numpy as jnp
from jax import lax
from jax.experimental import pallas as pl
from jax.experimental.pallas import tpu as pltpu
from jax.sharding import PartitionSpec as P

HEADS = 12
HEAD_DIM = 64
EPS = 1e-06
LIMITS = (12, 16, 23, 32, 46, 64, 91)
SCALE = 0.125
HIGH = lax.Precision.HIGHEST
LOW = jnp.bfloat16
FULL = jnp.float32
ROWS = 128
VMEM_BYTES = 52 * 1024 * 1024


def bucket_index(relative):
    distance = jnp.abs(relative)
    far_bucket = reduce(
        lambda counted, boundary: counted + (distance >= boundary).astype(jnp.int32),
        LIMITS,
        jnp.full_like(distance, 8),
    )
    return jnp.where(distance < 8, distance, far_bucket) + 16 * (relative > 0).astype(jnp.int32)


def segment_ids(lengths, slots):
    ending = jnp.cumsum(lengths)
    places = jnp.arange(slots, dtype=jnp.int32)
    return jnp.sum((places[:, None] >= ending[None, :]).astype(jnp.int32), axis=1)


def rms_parts(values, gain):
    inverse = lax.rsqrt(jnp.mean(values * values, axis=-1, keepdims=True) + EPS)
    return (values * inverse * gain, inverse)


def norm_back(values, inverse, gain, upstream):
    scaled = upstream * gain
    grad_values = inverse * scaled - values * inverse * inverse * inverse * jnp.mean(
        values * scaled, axis=-1, keepdims=True
    )
    return (grad_values, jnp.sum(upstream * values * inverse, axis=0))


def softmax_rows(scores):
    highest = jnp.max(scores, axis=-1, keepdims=True)
    raised = jnp.exp(scores - highest)
    return raised / jnp.sum(raised, axis=-1, keepdims=True)


def mm(left, right, contract, out=FULL):
    return lax.dot_general(left, right, (contract, ((), ())), preferred_element_type=FULL).astype(
        out
    )


def small_cost(flops, bytes_accessed, transcendentals):
    return pl.CostEstimate(
        flops=flops // 64,
        bytes_accessed=bytes_accessed // 64,
        transcendentals=transcendentals // 64,
    )


def nothing_kernel(*refs):
    del refs


def after(values, deps):
    values, deps = list(values), list(deps)
    anywhere = pl.BlockSpec(memory_space=pl.ANY)
    return pl.pallas_call(
        nothing_kernel,
        in_specs=[anywhere] * (len(values) + len(deps)),
        out_specs=[anywhere] * len(values),
        out_shape=[jax.ShapeDtypeStruct(value.shape, value.dtype) for value in values],
        input_output_aliases={number: number for number in range(len(values))},
        name="after",
    )(*values, *deps)


def swap(value, dim):
    axis, mask = dim
    count = lax.axis_size(axis)
    return lax.ppermute(value, axis, [(i, i ^ mask) for i in range(count)])


def bit_of(dim):
    axis, mask = dim
    return (lax.axis_index(axis) & mask) != 0


def stage_pair(value, dim):
    other = swap(value, dim)
    return jnp.where(bit_of(dim), jnp.stack((other, value)), jnp.stack((value, other)))


def ring_shift(value, places, by):
    count = 2 * places
    return lax.ppermute(value, "fsdp", [(i, (i - 2 * by) % count) for i in range(count)])


def z_gather(value, places, place):
    parts = jnp.stack([value] + [ring_shift(value, places, by) for by in range(1, places)])
    return lax.dynamic_slice_in_dim(
        jnp.concatenate((parts, parts)), lax.rem(places - place, places), places, 0
    )


def z_groups(places):
    return [[2 * place + side for place in range(places)] for side in (0, 1)]


def gather_step(held, dim):
    keys = list(held)
    value = jnp.stack([held[key] for key in keys]) if len(keys) > 1 else held[keys[0]]
    return swap(value, dim)


def gather_join(held, dim, arrived):
    keys = list(held)
    joined = dict(held)
    for number, key in enumerate(keys):
        joined[tuple(sorted(key + (dim,)))] = arrived[number] if len(keys) > 1 else arrived
    return joined


def gather_blocks(value, dims):
    held = {(): value}
    for dim in dims:
        held = gather_join(held, dim, gather_step(held, dim))
    return held


def gather_halves(value, dims):
    half = value.shape[0] // 2
    held = [{(): value[:half]}, {(): value[half:]}]
    brought = []
    for number in range(len(dims)):
        steps = (dims[number], dims[len(dims) - 1 - number])
        arrived = after([gather_step(part, dim) for part, dim in zip(held, steps)], ())
        brought.append(arrived)
        held = [gather_join(*of) for of in zip(held, steps, arrived)]
    upper, lower = held
    blocks = jnp.stack([jnp.concatenate((upper[key], lower[key])) for key in sorted(upper)])
    return (blocks, brought)


def scatter_halves(blocks, keys, dims):
    half = blocks.shape[1] // 2
    parts = [
        {key: blocks[number, :half] for number, key in enumerate(keys)},
        {key: blocks[number, half:] for number, key in enumerate(keys)},
    ]
    for number in range(len(dims)):
        steps = (dims[len(dims) - 1 - number], dims[number])
        stay = [[key for key in held if dim not in key] for held, dim in zip(parts, steps)]
        sent = [
            jnp.stack([held[tuple(sorted(key + (dim,)))].astype(LOW) for key in some])
            for held, dim, some in zip(parts, steps, stay)
        ]
        arrived = after([swap(value, dim) for value, dim in zip(sent, steps)], ())
        parts = [
            {
                key: held[key].astype(FULL) + value[place].astype(FULL)
                for place, key in enumerate(some)
            }
            for held, value, some in zip(parts, arrived, stay)
        ]
    return jnp.concatenate((parts[0][()], parts[1][()]))


def dense_gather(value, places, place, dims, core):
    columns = value.shape[1]
    half = (columns // 256) * 128
    near = z_gather(value, places, place)
    wanted = ("z", dims[0]) + tuple(sorted(dims[1:], reverse=True)) + ("core", "rows", "columns")

    def run(part, order):
        axes = ("z", "rows", "columns")
        for dim in order:
            part = stage_pair(part, dim)
            axes = (dim,) + axes
        part = stage_pair(part, core)
        axes = ("core",) + axes
        return part.transpose([axes.index(name) for name in wanted]).reshape(-1, part.shape[-1])

    first = run(near[..., :half], dims)
    second = run(near[..., half:], list(reversed(dims)))
    return (jnp.concatenate((first, second), axis=1), near)


def halve(parts, all_names, dims, beside=()):
    kept, sent, left = [], [], []
    for part, names, dim in zip(parts, all_names, dims):
        spot = names.index(dim)
        own = bit_of(dim).astype(jnp.int32)
        kept.append(lax.dynamic_index_in_dim(part, own, spot, keepdims=False))
        send = lax.dynamic_index_in_dim(part, 1 - own, spot, keepdims=False)
        sent.append(swap(send, dim))
        left.append(names[:spot] + names[spot + 1 :])
    arrived = after(sent + list(beside), ())
    sums = [(a.astype(FULL) + b.astype(FULL)).astype(LOW) for a, b in zip(kept, arrived)]
    return (sums, left, arrived[len(sent) :])


def add_up(value, others):
    return reduce(lambda total, other: total + other, others, value)


def dense_scatter(parts, names, orders, groups, small):
    all_names = [names] * len(parts)
    places = len(groups[0])
    for number, dims in enumerate(zip(*orders)):
        beside = ()
        if number == 0:
            beside = [swap(small, ("dp", mask)) for mask in range(1, lax.axis_size("dp"))]
        elif number == 1:
            beside = [swap(small, ("fsdp", 1))]
        parts, all_names, others = halve(parts, all_names, dims, beside)
        small = add_up(small, others)
    joined = jnp.concatenate(parts, axis=-1)
    moved = lax.all_to_all(
        joined, "fsdp", split_axis=0, concat_axis=0, axis_index_groups=groups, tiled=True
    )
    near = [ring_shift(small, places, by) for by in range(1, places)]
    moved, *others = after([moved] + near, ())
    return (jnp.sum(moved.astype(FULL), axis=0), add_up(small, others))


def diagonal_hot(slots, bucket_count):
    width = 2 * slots
    lanes = jnp.arange(width, dtype=jnp.int32)[None, :]
    rows = jnp.arange(8, dtype=jnp.int32)[:, None]
    diagonal = (lanes - rows + (ROWS - 1)) % width
    bucket = jnp.where(diagonal < width - 1, bucket_index(diagonal - (slots - 1)), -1)
    return (bucket[:, :, None] == jnp.arange(bucket_count, dtype=jnp.int32)).astype(FULL)


def attend_kernel(query, key, value, base, seg_col, seg_row, out, probs, toeplitz):
    slots = query.shape[0]
    lanes = lax.broadcasted_iota(jnp.int32, (1, 2 * HEAD_DIM), 1)
    total = [None] * (slots // ROWS)
    for head in range(2):
        mine = (lanes >= head * HEAD_DIM) & (lanes < (head + 1) * HEAD_DIM)
        table = base[head]
        size = 8
        while size < ROWS:
            table = jnp.concatenate((table, pltpu.roll(table, size, 1)), axis=0)
            size *= 2
        toeplitz[...] = table
        value_head = jnp.where(mine, value[...], 0).astype(LOW)
        for block in range(slots // ROWS):
            rows = pl.ds(block * ROWS, ROWS)
            query_head = jnp.where(mine, query[rows, :], 0).astype(LOW)
            shift = slots - ROWS - block * ROWS
            scores = mm(query_head, key[...], ((1,), (1,))) * SCALE
            scores = scores + toeplitz[:, shift : shift + slots]
            scores = jnp.where(seg_col[rows, :] == seg_row[...], scores, -1e30)
            highest = jnp.max(scores, axis=-1, keepdims=True)
            raised = jnp.exp(scores - highest)
            low = (raised / jnp.sum(raised, axis=-1, keepdims=True)).astype(LOW)
            probs[head, rows, :] = low
            part = mm(low, value_head, ((1,), (0,)))
            total[block] = part if head == 0 else total[block] + part
    for block in range(slots // ROWS):
        out[pl.ds(block * ROWS, ROWS), :] = total[block].astype(LOW)


def attend_forward(projected, base, seg_col, seg_row):
    slots = projected.shape[0]
    width = projected.shape[1] // 3
    pairs = HEADS // 2
    lanes = 2 * HEAD_DIM
    return pl.pallas_call(
        attend_kernel,
        grid=(pairs,),
        in_specs=[
            pl.BlockSpec((slots, lanes), lambda p: (0, p)),
            pl.BlockSpec((slots, lanes), lambda p: (0, p + pairs)),
            pl.BlockSpec((slots, lanes), lambda p: (0, p + 2 * pairs)),
            pl.BlockSpec((2, 8, 2 * slots), lambda p: (p, 0, 0)),
            pl.BlockSpec((slots, 1), lambda p: (0, 0)),
            pl.BlockSpec((1, slots), lambda p: (0, 0)),
        ],
        out_specs=[
            pl.BlockSpec((slots, lanes), lambda p: (0, p)),
            pl.BlockSpec((2, slots, slots), lambda p: (p, 0, 0)),
        ],
        out_shape=[
            jax.ShapeDtypeStruct((slots, width), LOW),
            jax.ShapeDtypeStruct((HEADS, slots, slots), LOW),
        ],
        scratch_shapes=[pltpu.VMEM((ROWS, 2 * slots), FULL)],
        compiler_params=pltpu.CompilerParams(vmem_limit_bytes=VMEM_BYTES),
        cost_estimate=small_cost(
            flops=HEADS * slots * slots * HEAD_DIM * 16,
            bytes_accessed=HEADS * slots * slots * 2 + 8 * slots * width,
            transcendentals=HEADS * slots * slots,
        ),
        name="attend_forward",
    )(projected, projected, projected, base, seg_col, seg_row)


def attend_back_kernel(
    query, key, value, grad, probs, out_query, out_key, out_value, diagonals, lined, scores_low
):
    slots = query.shape[0]
    lanes = lax.broadcasted_iota(jnp.int32, (1, 2 * HEAD_DIM), 1)
    query_total = [None] * (slots // ROWS)
    key_total = value_total = None
    for head in range(2):
        mine = (lanes >= head * HEAD_DIM) & (lanes < (head + 1) * HEAD_DIM)
        key_head = jnp.where(mine, key[...], 0).astype(LOW)
        grad_head = jnp.where(mine, grad[...], 0).astype(LOW)
        query_head = jnp.where(mine, query[...], 0).astype(LOW)
        lined[...] = jnp.zeros_like(lined)
        for block in range(slots // ROWS):
            rows = pl.ds(block * ROWS, ROWS)
            soft = probs[head, rows, :].astype(FULL)
            grad_rows = jnp.where(mine, grad[rows, :], 0).astype(LOW)
            weighted = soft * mm(grad_rows, value[...], ((1,), (1,)))
            back = weighted - soft * jnp.sum(weighted, axis=-1, keepdims=True)
            low = back.astype(LOW)
            scores_low[rows, :] = low
            shift = slots - ROWS - block * ROWS
            lined[:, shift : shift + slots] += low.astype(FULL)
            part = mm(low, key_head, ((1,), (0,)))
            query_total[block] = part if head == 0 else query_total[block] + part
        key_part = mm(scores_low[...], query_head, ((0,), (0,)))
        value_part = mm(probs[head], grad_head, ((0,), (0,)))
        key_total = key_part if head == 0 else key_total + key_part
        value_total = value_part if head == 0 else value_total + value_part
        table = lined[...]
        size = ROWS
        while size > 8:
            size //= 2
            table = table[:size] + pltpu.roll(table[size:], 2 * slots - size, 1)
        diagonals[head] = table
    out_key[...] = (key_total * SCALE).astype(LOW)
    out_value[...] = value_total.astype(LOW)
    for block in range(slots // ROWS):
        out_query[pl.ds(block * ROWS, ROWS), :] = (query_total[block] * SCALE).astype(LOW)


def attend_back(projected, grad_attended, probs, begin, count):
    slots = projected.shape[0]
    pairs = HEADS // 2
    lanes = 2 * HEAD_DIM
    width = count * lanes
    column = pl.BlockSpec((slots, lanes), lambda p: (0, p))

    def column_from(offset):
        return pl.BlockSpec((slots, lanes), lambda p: (0, p + offset))

    return pl.pallas_call(
        attend_back_kernel,
        grid=(count,),
        in_specs=[
            column_from(begin),
            column_from(begin + pairs),
            column_from(begin + 2 * pairs),
            column_from(begin),
            pl.BlockSpec((2, slots, slots), lambda p: (p + begin, 0, 0)),
        ],
        out_specs=[
            column,
            column,
            column,
            pl.BlockSpec((2, 8, 2 * slots), lambda p: (p, 0, 0)),
        ],
        out_shape=[jax.ShapeDtypeStruct((slots, width), LOW)] * 3
        + [jax.ShapeDtypeStruct((2 * count, 8, 2 * slots), FULL)],
        scratch_shapes=[pltpu.VMEM((ROWS, 2 * slots), FULL), pltpu.VMEM((slots, slots), LOW)],
        compiler_params=pltpu.CompilerParams(vmem_limit_bytes=VMEM_BYTES),
        cost_estimate=small_cost(
            flops=2 * count * slots * slots * HEAD_DIM * 32,
            bytes_accessed=2 * count * slots * slots * 2 + 14 * slots * width,
            transcendentals=0,
        ),
        name="attend_back",
    )(projected, projected, projected, grad_attended, probs)


def second_of(weights):
    _, rows, units = weights.shape
    width = rows // 2
    runs = [weights[0, row : row + units, :] for row in range(width, rows, units)]
    return jnp.concatenate(runs, axis=1)


def expert_kernel(
    rows, grads, weights, y_out, back_out, weights_out, y_sum, back_sum, hidden_low, pre_low
):
    chunk = pl.program_id(0)
    count, width = rows.shape[1:]
    units = weights.shape[2]
    step = min(256, count)
    second = second_of(weights)

    @pl.when(chunk == 0)
    def _():
        y_sum[...] = jnp.zeros_like(y_sum)
        back_sum[...] = jnp.zeros_like(back_sum)

    for block in range(count // step):
        some = pl.ds(block * step, step)
        pre = mm(rows[0, some, :], weights[0, :width, :], ((1,), (0,)))
        grad_hidden = mm(grads[0, some, :], second, ((1,), (1,)))
        normal_cdf = 0.5 + 0.5 * lax.erf(pre * 0.7071067811865476)
        slope = normal_cdf + pre * jnp.exp(-0.5 * pre * pre) * 0.3989422804014327
        hidden = (pre * normal_cdf).astype(LOW)
        grad_pre = (grad_hidden * slope).astype(LOW)
        hidden_low[some, :] = hidden
        pre_low[some, :] = grad_pre
        y_sum[some, :] += mm(hidden, second, ((1,), (0,)))
        back_sum[some, :] += mm(grad_pre, weights[0, :width, :], ((1,), (1,)))
    weights_out[0, :width, :] = mm(rows[0], pre_low[...], ((0,), (0,)), LOW)
    second_grad = mm(hidden_low[...], grads[0], ((0,), (0,)), LOW)
    for column in range(0, width, units):
        weights_out[0, width + column : width + column + units, :] = second_grad[
            :, column : column + units
        ]

    @pl.when(chunk == pl.num_programs(0) - 1)
    def _():
        y_out[...] = y_sum[...].astype(LOW)
        back_out[...] = back_sum[...].astype(LOW)


def run_expert(expert, rows, grads, weights):
    chunks, height, units = weights.shape
    count, width = rows.shape[1:]
    rows_in = pl.BlockSpec((1, count, width), lambda c: (expert, 0, 0))
    rows_out = pl.BlockSpec((count, width), lambda c: (0, 0))
    weight_spec = pl.BlockSpec((1, height, units), lambda c: (c, 0, 0))
    rows_shape = jax.ShapeDtypeStruct((count, width), LOW)
    return pl.pallas_call(
        expert_kernel,
        grid=(chunks,),
        in_specs=[rows_in, rows_in, weight_spec],
        out_specs=[rows_out, rows_out, weight_spec],
        out_shape=[rows_shape, rows_shape, jax.ShapeDtypeStruct(weights.shape, LOW)],
        scratch_shapes=[
            pltpu.VMEM((count, width), FULL),
            pltpu.VMEM((count, width), FULL),
            pltpu.VMEM((count, units), LOW),
            pltpu.VMEM((count, units), LOW),
        ],
        compiler_params=pltpu.CompilerParams(vmem_limit_bytes=VMEM_BYTES),
        cost_estimate=small_cost(
            flops=chunks * 12 * count * width * units,
            bytes_accessed=8 * count * width + 8 * chunks * width * units,
            transcendentals=2 * chunks * count * units,
        ),
        name="run_expert",
    )(rows, grads, weights)


def place_kernel(groups, hot, *refs):
    *parts, out = refs
    size = len(parts) // groups
    width = parts[0].shape[1]
    for group in range(groups):
        some = [part[...] for part in parts[group * size : (group + 1) * size]]
        values = jnp.concatenate(some, axis=0)
        out[0, :, group * width : (group + 1) * width] = mm(hot[0], values, ((1,), (0,)), LOW)


def place_rows(hot, groups, capacity):
    blocks, count, slots = hot.shape
    parts = sum(groups, [])
    width = parts[0].shape[1]
    wide = width * len(groups)
    return pl.pallas_call(
        partial(place_kernel, len(groups)),
        grid=(blocks,),
        in_specs=[pl.BlockSpec((1, count, slots), lambda b: (b, 0, 0))]
        + [pl.BlockSpec((capacity, width), lambda b: (b, 0))] * len(parts),
        out_specs=pl.BlockSpec((1, count, wide), lambda b: (b, 0, 0)),
        out_shape=jax.ShapeDtypeStruct((blocks, count, wide), LOW),
        compiler_params=pltpu.CompilerParams(vmem_limit_bytes=VMEM_BYTES),
        cost_estimate=small_cost(
            flops=2 * blocks * count * slots * wide,
            bytes_accessed=4 * blocks * count * wide,
            transcendentals=0,
        ),
        name="place_rows",
    )(hot, *parts)


def body(
    tokens,
    cotangent,
    seq_lens,
    routes,
    norm_gains,
    qkv_weight,
    out_weight,
    router_weight,
    rel_bias,
    expert_in,
    expert_out,
):
    tok_count, width = tokens.shape
    bucket_count = rel_bias.shape[0]
    shard_rows = qkv_weight.shape[0]
    experts_all = router_weight.shape[1]
    local_experts, _, units = expert_in.shape
    capacity = 2 * tok_count // experts_all
    places = lax.axis_size("fsdp") // 2
    place = lax.axis_index("fsdp") // 2
    peer = lax.axis_index("dp")
    peer_count = lax.axis_size("dp")
    core = ("dp", 1)
    dims = [("fsdp", 1)]
    mask = 2
    while mask < peer_count:
        dims.append(("dp", mask))
        mask *= 2

    spare = -(4 * width + experts_all + 2) % 128
    packed = jnp.concatenate(
        (
            qkv_weight,
            out_weight,
            router_weight,
            norm_gains.T,
            jnp.zeros((shard_rows, spare), LOW),
        ),
        axis=1,
    )
    dense, near = dense_gather(packed, places, place, dims, core)
    qkv_full = dense[:, : 3 * width]
    out_full = dense[:, 3 * width : 4 * width]
    router_full = dense[:, 4 * width : 4 * width + experts_all]
    gains_float = dense[:, 4 * width + experts_all : 4 * width + experts_all + 2].T.astype(FULL)

    groups = z_groups(places)
    weights = []
    for expert in range(local_experts):
        runs = [expert_out[expert][:, row : row + units] for row in range(0, width, units)]
        own = jnp.concatenate([expert_in[expert]] + runs)
        if expert > 0:
            (own,) = after((own,), (near,))
        weights.append(lax.all_gather(own, "fsdp", axis=0, axis_index_groups=groups))

    chosen = routes[:, 0]
    chosen_hot = chosen[:, None] == jnp.arange(experts_all, dtype=jnp.int32)[None, :]
    order = jnp.arange(tok_count, dtype=jnp.int32)
    earlier = (order[:, None] > order[None, :]).astype(LOW)
    rank_all = jnp.dot(earlier, chosen_hot.astype(LOW), preferred_element_type=FULL)
    rank_in = jnp.sum(jnp.where(chosen_hot, rank_all, 0.0), axis=1).astype(jnp.int32)
    slots_of = gather_blocks((chosen * capacity + rank_in)[None, :], dims)
    keys = sorted(slots_of)
    slots_near = jnp.stack([slots_of[key][0] for key in keys])
    local_slots = local_experts * capacity
    slot_ids = jnp.arange(local_slots, dtype=jnp.int32).reshape(local_experts, capacity)

    def hot_of(owner):
        wanted = owner * local_slots + slot_ids
        return (slots_near[:, None, None, :] == wanted[None, :, :, None]).astype(LOW)

    hot_own, hot_other = hot_of(peer), hot_of(peer ^ 1)
    segment = segment_ids(seq_lens[0], tok_count)
    bucket_hot = diagonal_hot(tok_count, bucket_count)
    base = jnp.einsum("rjb,bh->hrj", bucket_hot, rel_bias, precision=HIGH)

    inputs = tokens.astype(FULL)
    normed_one, inverse_one = rms_parts(inputs, gains_float[0])
    normed_low = normed_one.astype(LOW)
    projected = jnp.dot(normed_low, qkv_full, preferred_element_type=FULL).astype(LOW)
    attended, probs = attend_forward(projected, base, segment[:, None], segment[None, :])
    hidden_one = inputs + jnp.dot(attended, out_full, preferred_element_type=FULL)
    normed_two, inverse_two = rms_parts(hidden_one, gains_float[1])
    normed_two_low = normed_two.astype(LOW)
    router_soft = softmax_rows(jnp.dot(normed_two_low, router_full, preferred_element_type=FULL))
    gate_value = jnp.sum(jnp.where(chosen_hot, router_soft, 0.0), axis=1)
    upstream = cotangent.astype(FULL)
    grad_y = (gate_value[:, None] * upstream).astype(LOW)

    def pick(hot, blocks):
        return jnp.einsum("bjst,btd->jbsd", hot, blocks, preferred_element_type=FULL).astype(LOW)

    def to_rows(blocks):
        other = swap(pick(hot_other, blocks), core)
        both = jnp.stack((pick(hot_own, blocks), other), axis=1)
        return both.reshape(local_experts, -1, width)

    token_ids = jnp.concatenate((peer * local_slots + slot_ids, (peer ^ 1) * local_slots + slot_ids))
    hot_back = (slots_near[:, :, None] == token_ids.reshape(-1)[None, None, :]).astype(LOW)

    def from_rows(*groups):
        near_rows = len(keys) * capacity
        parts = [
            list(values) + [swap(value[near_rows:], core) for value in values] for values in groups
        ]
        return place_rows(hot_back, parts, capacity)

    blocks, brought = gather_halves(normed_two_low, dims)
    rows = to_rows(blocks)
    (grad_tied,) = after((grad_y,), brought[0])
    grad_blocks, _ = gather_halves(grad_tied, dims)
    grads = to_rows(grad_blocks)
    results = []
    for expert in range(local_experts):
        held = weights[expert]
        if expert > 0:
            (held,) = after((held,), (results[-1][0], hot_back))
        results.append(run_expert(expert, rows, grads, held))
    summed = [
        lax.psum_scatter(
            result[2], "fsdp", scatter_dimension=0, axis_index_groups=groups, tiled=False
        )
        for result in results
    ]
    returned = scatter_halves(
        from_rows(*[[result[which] for result in results] for which in (0, 1)]), keys, dims
    )
    token_y, grad_rows = returned[:, :width], returned[:, width:]

    mixed = (hidden_one + gate_value[:, None] * token_y).astype(LOW)
    grad_gate = jnp.sum(upstream * token_y, axis=1)
    grad_logits = router_soft * (
        jnp.where(chosen_hot, grad_gate[:, None], 0.0) - (gate_value * grad_gate)[:, None]
    )
    router_local = jnp.dot(normed_two_low.astype(FULL).T, grad_logits, precision=HIGH)
    grad_normed_two = grad_rows + jnp.dot(
        grad_logits, router_full.astype(FULL).T, precision=HIGH
    )
    grad_from_two, gain_grad_two = norm_back(
        hidden_one, inverse_two, gains_float[1], grad_normed_two
    )
    grad_hidden_one = upstream + grad_from_two
    grad_attn_low = grad_hidden_one.astype(LOW)
    out_local = jnp.einsum("td,te->de", attended, grad_attn_low, preferred_element_type=FULL)
    grad_attended = mm(grad_attn_low, out_full, ((1,), (1,)), LOW)
    names = ["z", dims[0]] + sorted(dims[1:], reverse=True) + [core]

    def split_rows(panel):
        shape = (places,) + (2,) * (len(names) - 1) + (shard_rows, panel.shape[1])
        parts, left, _ = halve([panel.reshape(shape)], [names], [core])
        return (parts[0], left[0])

    spare_out = -(experts_all + 2) % 128
    out_panel = jnp.concatenate(
        (
            out_local.astype(LOW),
            router_local.astype(LOW),
            gain_grad_two[:, None].astype(LOW),
            jnp.zeros((width, spare_out + 1), LOW),
        ),
        axis=1,
    )
    out_half, half_names = split_rows(out_panel)
    early = summed[:-1]
    (grad_attended,) = after((grad_attended,), early)
    *grad_parts, diagonals = attend_back(projected, grad_attended, probs, 0, HEADS // 2)
    grad_projected = jnp.concatenate(grad_parts, axis=1)
    qkv_local = mm(normed_low, grad_projected, ((0,), (0,)), LOW)
    qkv_half, _ = split_rows(qkv_local)
    half = 3 * width // 2
    grad_normed_one = mm(grad_projected, qkv_full, ((1,), (1,)))
    grad_from_one, gain_grad_one = norm_back(inputs, inverse_one, gains_float[0], grad_normed_one)
    tokens_grad = grad_hidden_one + grad_from_one
    bias_local = jnp.einsum("hrj,rjb->bh", diagonals, bucket_hot, precision=HIGH)
    gain_rows = width // 128
    small = jnp.concatenate((bias_local.reshape(-1, 128), gain_grad_one.reshape(-1, 128)))
    dense_sum, small = dense_scatter(
        [qkv_half[..., :half], qkv_half[..., half:], out_half],
        half_names,
        [dims, dims[::-1], dims[::-1]],
        groups,
        small,
    )
    summed[-1:] = after(summed[-1:], (dense_sum,))
    in_grad = jnp.stack([both[:width].astype(FULL) for both in summed])
    out_expert_grad = jnp.stack(
        [
            jnp.concatenate(
                [both[row : row + units].astype(FULL) for row in range(width, 2 * width, units)],
                axis=1,
            )
            for both in summed
        ]
    )
    qkv_grad, out_sum = dense_sum[:, : 3 * width], dense_sum[:, 3 * width :]
    bias_grad = small[:-gain_rows].reshape(bias_local.shape)
    device = lax.axis_index("fsdp") * peer_count + peer
    gain_one = lax.dynamic_slice_in_dim(
        small[-gain_rows:].reshape(-1), device * shard_rows, shard_rows
    )
    gains_grad = jnp.stack((gain_one, out_sum[:, width + experts_all]))
    router_grad = out_sum[:, width : width + experts_all]
    out_grad = out_sum[:, :width]
    return (
        mixed,
        tokens_grad,
        gains_grad,
        qkv_grad,
        out_grad,
        router_grad,
        bias_grad,
        in_grad,
        out_expert_grad,
    )


def solution(mesh):
    rows = P(("fsdp", "dp"), None)
    columns = P(None, ("fsdp", "dp"))
    experts = (P("dp", None, "fsdp"), P("dp", "fsdp", None))
    return jax.shard_map(
        body,
        mesh=mesh,
        in_specs=(rows, rows, rows, rows, columns, rows, rows, rows, P()) + experts,
        out_specs=(rows, rows, columns, rows, rows, rows, P()) + experts,
        check_vma=False,
    )
```

```python
from functools import partial, reduce

import jax
import jax.numpy as jnp
from jax import lax
from jax.experimental import pallas as pl
from jax.experimental.pallas import tpu as pltpu
from jax.sharding import PartitionSpec as P

HEADS = 12
HEAD_DIM = 64
EPS = 1e-06
LIMITS = (12, 16, 23, 32, 46, 64, 91)
SCALE = 0.125
HIGH = lax.Precision.HIGHEST
LOW = jnp.bfloat16
FULL = jnp.float32
ROWS = 128
VMEM_BYTES = 52 * 1024 * 1024


def bucket_index(relative):
    distance = jnp.abs(relative)
    far_bucket = reduce(
        lambda counted, boundary: counted + (distance >= boundary).astype(jnp.int32),
        LIMITS,
        jnp.full_like(distance, 8),
    )
    return jnp.where(distance < 8, distance, far_bucket) + 16 * (relative > 0).astype(jnp.int32)


def segment_ids(lengths, slots):
    ending = jnp.cumsum(lengths)
    places = jnp.arange(slots, dtype=jnp.int32)
    return jnp.sum((places[:, None] >= ending[None, :]).astype(jnp.int32), axis=1)


def rms_parts(values, gain):
    inverse = lax.rsqrt(jnp.mean(values * values, axis=-1, keepdims=True) + EPS)
    return (values * inverse * gain, inverse)


def norm_back(values, inverse, gain, upstream):
    scaled = upstream * gain
    grad_values = inverse * scaled - values * inverse * inverse * inverse * jnp.mean(
        values * scaled, axis=-1, keepdims=True
    )
    return (grad_values, jnp.sum(upstream * values * inverse, axis=0))


def softmax_rows(scores):
    highest = jnp.max(scores, axis=-1, keepdims=True)
    raised = jnp.exp(scores - highest)
    return raised / jnp.sum(raised, axis=-1, keepdims=True)


def mm(left, right, contract, out=FULL):
    return lax.dot_general(left, right, (contract, ((), ())), preferred_element_type=FULL).astype(
        out
    )


def small_cost(flops, bytes_accessed, transcendentals):
    return pl.CostEstimate(
        flops=flops // 64,
        bytes_accessed=bytes_accessed // 64,
        transcendentals=transcendentals // 64,
    )


def nothing_kernel(*refs):
    del refs


def after(values, deps):
    values, deps = list(values), list(deps)
    anywhere = pl.BlockSpec(memory_space=pl.ANY)
    return pl.pallas_call(
        nothing_kernel,
        in_specs=[anywhere] * (len(values) + len(deps)),
        out_specs=[anywhere] * len(values),
        out_shape=[jax.ShapeDtypeStruct(value.shape, value.dtype) for value in values],
        input_output_aliases={number: number for number in range(len(values))},
        name="after",
    )(*values, *deps)


def swap(value, dim):
    axis, mask = dim
    count = lax.axis_size(axis)
    return lax.ppermute(value, axis, [(i, i ^ mask) for i in range(count)])


def bit_of(dim):
    axis, mask = dim
    return (lax.axis_index(axis) & mask) != 0


def stage_pair(value, dim):
    other = swap(value, dim)
    return jnp.where(bit_of(dim), jnp.stack((other, value)), jnp.stack((value, other)))


def ring_shift(value, places, by):
    count = 2 * places
    return lax.ppermute(value, "fsdp", [(i, (i - 2 * by) % count) for i in range(count)])


def z_gather(value, places, place):
    parts = jnp.stack([value] + [ring_shift(value, places, by) for by in range(1, places)])
    return lax.dynamic_slice_in_dim(
        jnp.concatenate((parts, parts)), lax.rem(places - place, places), places, 0
    )


def z_groups(places):
    return [[2 * place + side for place in range(places)] for side in (0, 1)]


def gather_step(held, dim):
    keys = list(held)
    value = jnp.stack([held[key] for key in keys]) if len(keys) > 1 else held[keys[0]]
    return swap(value, dim)


def gather_join(held, dim, arrived):
    keys = list(held)
    joined = dict(held)
    for number, key in enumerate(keys):
        joined[tuple(sorted(key + (dim,)))] = arrived[number] if len(keys) > 1 else arrived
    return joined


def gather_blocks(value, dims):
    held = {(): value}
    for dim in dims:
        held = gather_join(held, dim, gather_step(held, dim))
    return held


def gather_halves(value, dims):
    half = value.shape[0] // 2
    held = [{(): value[:half]}, {(): value[half:]}]
    brought = []
    for number in range(len(dims)):
        steps = (dims[number], dims[len(dims) - 1 - number])
        arrived = after([gather_step(part, dim) for part, dim in zip(held, steps)], ())
        brought.append(arrived)
        held = [gather_join(*of) for of in zip(held, steps, arrived)]
    upper, lower = held
    blocks = jnp.stack([jnp.concatenate((upper[key], lower[key])) for key in sorted(upper)])
    return (blocks, brought)


def scatter_halves(blocks, keys, dims):
    half = blocks.shape[1] // 2
    parts = [
        {key: blocks[number, :half] for number, key in enumerate(keys)},
        {key: blocks[number, half:] for number, key in enumerate(keys)},
    ]
    for number in range(len(dims)):
        steps = (dims[len(dims) - 1 - number], dims[number])
        stay = [[key for key in held if dim not in key] for held, dim in zip(parts, steps)]
        sent = [
            jnp.stack([held[tuple(sorted(key + (dim,)))].astype(LOW) for key in some])
            for held, dim, some in zip(parts, steps, stay)
        ]
        arrived = after([swap(value, dim) for value, dim in zip(sent, steps)], ())
        parts = [
            {
                key: held[key].astype(FULL) + value[place].astype(FULL)
                for place, key in enumerate(some)
            }
            for held, value, some in zip(parts, arrived, stay)
        ]
    return jnp.concatenate((parts[0][()], parts[1][()]))


def dense_gather(value, places, place, dims, core):
    columns = value.shape[1]
    half = (columns // 256) * 128
    near = z_gather(value, places, place)
    wanted = ("z", dims[0]) + tuple(sorted(dims[1:], reverse=True)) + ("core", "rows", "columns")

    def run(part, order):
        axes = ("z", "rows", "columns")
        for dim in order:
            part = stage_pair(part, dim)
            axes = (dim,) + axes
        part = stage_pair(part, core)
        axes = ("core",) + axes
        return part.transpose([axes.index(name) for name in wanted]).reshape(-1, part.shape[-1])

    first = run(near[..., :half], dims)
    second = run(near[..., half:], list(reversed(dims)))
    return (jnp.concatenate((first, second), axis=1), near)


def halve(parts, all_names, dims, beside=()):
    kept, sent, left = [], [], []
    for part, names, dim in zip(parts, all_names, dims):
        spot = names.index(dim)
        own = bit_of(dim).astype(jnp.int32)
        kept.append(lax.dynamic_index_in_dim(part, own, spot, keepdims=False))
        send = lax.dynamic_index_in_dim(part, 1 - own, spot, keepdims=False)
        sent.append(swap(send, dim))
        left.append(names[:spot] + names[spot + 1 :])
    arrived = after(sent + list(beside), ())
    sums = [(a.astype(FULL) + b.astype(FULL)).astype(LOW) for a, b in zip(kept, arrived)]
    return (sums, left, arrived[len(sent) :])


def add_up(value, others):
    return reduce(lambda total, other: total + other, others, value)


def dense_scatter(parts, names, orders, groups, small):
    all_names = [names] * len(parts)
    places = len(groups[0])
    for number, dims in enumerate(zip(*orders)):
        beside = ()
        if number == 0:
            beside = [swap(small, ("dp", mask)) for mask in range(1, lax.axis_size("dp"))]
        elif number == 1:
            beside = [swap(small, ("fsdp", 1))]
        parts, all_names, others = halve(parts, all_names, dims, beside)
        small = add_up(small, others)
    joined = jnp.concatenate(parts, axis=-1)
    moved = lax.all_to_all(
        joined, "fsdp", split_axis=0, concat_axis=0, axis_index_groups=groups, tiled=True
    )
    near = [ring_shift(small, places, by) for by in range(1, places)]
    moved, *others = after([moved] + near, ())
    return (jnp.sum(moved.astype(FULL), axis=0), add_up(small, others))


def diagonal_hot(slots, bucket_count):
    width = 2 * slots
    lanes = jnp.arange(width, dtype=jnp.int32)[None, :]
    rows = jnp.arange(8, dtype=jnp.int32)[:, None]
    diagonal = (lanes - rows + (ROWS - 1)) % width
    bucket = jnp.where(diagonal < width - 1, bucket_index(diagonal - (slots - 1)), -1)
    return (bucket[:, :, None] == jnp.arange(bucket_count, dtype=jnp.int32)).astype(FULL)


def attend_kernel(query, key, value, base, seg_col, seg_row, out, probs, toeplitz):
    slots = query.shape[0]
    lanes = lax.broadcasted_iota(jnp.int32, (1, 2 * HEAD_DIM), 1)
    total = [None] * (slots // ROWS)
    for head in range(2):
        mine = (lanes >= head * HEAD_DIM) & (lanes < (head + 1) * HEAD_DIM)
        table = base[head]
        size = 8
        while size < ROWS:
            table = jnp.concatenate((table, pltpu.roll(table, size, 1)), axis=0)
            size *= 2
        toeplitz[...] = table
        value_head = jnp.where(mine, value[...], 0).astype(LOW)
        for block in range(slots // ROWS):
            rows = pl.ds(block * ROWS, ROWS)
            query_head = jnp.where(mine, query[rows, :], 0).astype(LOW)
            shift = slots - ROWS - block * ROWS
            scores = mm(query_head, key[...], ((1,), (1,))) * SCALE
            scores = scores + toeplitz[:, shift : shift + slots]
            scores = jnp.where(seg_col[rows, :] == seg_row[...], scores, -1e30)
            highest = jnp.max(scores, axis=-1, keepdims=True)
            raised = jnp.exp(scores - highest)
            low = (raised / jnp.sum(raised, axis=-1, keepdims=True)).astype(LOW)
            probs[head, rows, :] = low
            part = mm(low, value_head, ((1,), (0,)))
            total[block] = part if head == 0 else total[block] + part
    for block in range(slots // ROWS):
        out[pl.ds(block * ROWS, ROWS), :] = total[block].astype(LOW)


def attend_forward(projected, base, seg_col, seg_row):
    slots = projected.shape[0]
    width = projected.shape[1] // 3
    pairs = HEADS // 2
    lanes = 2 * HEAD_DIM
    return pl.pallas_call(
        attend_kernel,
        grid=(pairs,),
        in_specs=[
            pl.BlockSpec((slots, lanes), lambda p: (0, p)),
            pl.BlockSpec((slots, lanes), lambda p: (0, p + pairs)),
            pl.BlockSpec((slots, lanes), lambda p: (0, p + 2 * pairs)),
            pl.BlockSpec((2, 8, 2 * slots), lambda p: (p, 0, 0)),
            pl.BlockSpec((slots, 1), lambda p: (0, 0)),
            pl.BlockSpec((1, slots), lambda p: (0, 0)),
        ],
        out_specs=[
            pl.BlockSpec((slots, lanes), lambda p: (0, p)),
            pl.BlockSpec((2, slots, slots), lambda p: (p, 0, 0)),
        ],
        out_shape=[
            jax.ShapeDtypeStruct((slots, width), LOW),
            jax.ShapeDtypeStruct((HEADS, slots, slots), LOW),
        ],
        scratch_shapes=[pltpu.VMEM((ROWS, 2 * slots), FULL)],
        compiler_params=pltpu.CompilerParams(vmem_limit_bytes=VMEM_BYTES),
        cost_estimate=small_cost(
            flops=HEADS * slots * slots * HEAD_DIM * 16,
            bytes_accessed=HEADS * slots * slots * 2 + 8 * slots * width,
            transcendentals=HEADS * slots * slots,
        ),
        name="attend_forward",
    )(projected, projected, projected, base, seg_col, seg_row)


def attend_back_kernel(
    query, key, value, grad, probs, out_query, out_key, out_value, diagonals, lined, scores_low
):
    slots = query.shape[0]
    lanes = lax.broadcasted_iota(jnp.int32, (1, 2 * HEAD_DIM), 1)
    query_total = [None] * (slots // ROWS)
    key_total = value_total = None
    for head in range(2):
        mine = (lanes >= head * HEAD_DIM) & (lanes < (head + 1) * HEAD_DIM)
        key_head = jnp.where(mine, key[...], 0).astype(LOW)
        grad_head = jnp.where(mine, grad[...], 0).astype(LOW)
        query_head = jnp.where(mine, query[...], 0).astype(LOW)
        lined[...] = jnp.zeros_like(lined)
        for block in range(slots // ROWS):
            rows = pl.ds(block * ROWS, ROWS)
            soft = probs[head, rows, :].astype(FULL)
            grad_rows = jnp.where(mine, grad[rows, :], 0).astype(LOW)
            weighted = soft * mm(grad_rows, value[...], ((1,), (1,)))
            back = weighted - soft * jnp.sum(weighted, axis=-1, keepdims=True)
            low = back.astype(LOW)
            scores_low[rows, :] = low
            shift = slots - ROWS - block * ROWS
            lined[:, shift : shift + slots] += low.astype(FULL)
            part = mm(low, key_head, ((1,), (0,)))
            query_total[block] = part if head == 0 else query_total[block] + part
        key_part = mm(scores_low[...], query_head, ((0,), (0,)))
        value_part = mm(probs[head], grad_head, ((0,), (0,)))
        key_total = key_part if head == 0 else key_total + key_part
        value_total = value_part if head == 0 else value_total + value_part
        table = lined[...]
        size = ROWS
        while size > 8:
            size //= 2
            table = table[:size] + pltpu.roll(table[size:], 2 * slots - size, 1)
        diagonals[head] = table
    out_key[...] = (key_total * SCALE).astype(LOW)
    out_value[...] = value_total.astype(LOW)
    for block in range(slots // ROWS):
        out_query[pl.ds(block * ROWS, ROWS), :] = (query_total[block] * SCALE).astype(LOW)


def attend_back(projected, grad_attended, probs, begin, count):
    slots = projected.shape[0]
    pairs = HEADS // 2
    lanes = 2 * HEAD_DIM
    width = count * lanes
    column = pl.BlockSpec((slots, lanes), lambda p: (0, p))

    def column_from(offset):
        return pl.BlockSpec((slots, lanes), lambda p: (0, p + offset))

    return pl.pallas_call(
        attend_back_kernel,
        grid=(count,),
        in_specs=[
            column_from(begin),
            column_from(begin + pairs),
            column_from(begin + 2 * pairs),
            column_from(begin),
            pl.BlockSpec((2, slots, slots), lambda p: (p + begin, 0, 0)),
        ],
        out_specs=[
            column,
            column,
            column,
            pl.BlockSpec((2, 8, 2 * slots), lambda p: (p, 0, 0)),
        ],
        out_shape=[jax.ShapeDtypeStruct((slots, width), LOW)] * 3
        + [jax.ShapeDtypeStruct((2 * count, 8, 2 * slots), FULL)],
        scratch_shapes=[pltpu.VMEM((ROWS, 2 * slots), FULL), pltpu.VMEM((slots, slots), LOW)],
        compiler_params=pltpu.CompilerParams(vmem_limit_bytes=VMEM_BYTES),
        cost_estimate=small_cost(
            flops=2 * count * slots * slots * HEAD_DIM * 32,
            bytes_accessed=2 * count * slots * slots * 2 + 14 * slots * width,
            transcendentals=0,
        ),
        name="attend_back",
    )(projected, projected, projected, grad_attended, probs)


def second_of(weights):
    _, rows, units = weights.shape
    width = rows // 2
    runs = [weights[0, row : row + units, :] for row in range(width, rows, units)]
    return jnp.concatenate(runs, axis=1)


def expert_kernel(
    rows, grads, weights, y_out, back_out, weights_out, y_sum, back_sum, hidden_low, pre_low
):
    chunk = pl.program_id(0)
    count, width = rows.shape[1:]
    units = weights.shape[2]
    step = min(512, count)
    second = second_of(weights)

    @pl.when(chunk == 0)
    def _():
        y_sum[...] = jnp.zeros_like(y_sum)
        back_sum[...] = jnp.zeros_like(back_sum)

    for block in range(count // step):
        some = pl.ds(block * step, step)
        pre = mm(rows[0, some, :], weights[0, :width, :], ((1,), (0,)))
        grad_hidden = mm(grads[0, some, :], second, ((1,), (1,)))
        normal_cdf = 0.5 + 0.5 * lax.erf(pre * 0.7071067811865476)
        slope = normal_cdf + pre * jnp.exp(-0.5 * pre * pre) * 0.3989422804014327
        hidden = (pre * normal_cdf).astype(LOW)
        grad_pre = (grad_hidden * slope).astype(LOW)
        hidden_low[some, :] = hidden
        pre_low[some, :] = grad_pre
        y_sum[some, :] += mm(hidden, second, ((1,), (0,)))
        back_sum[some, :] += mm(grad_pre, weights[0, :width, :], ((1,), (1,)))
    weights_out[0, :width, :] = mm(rows[0], pre_low[...], ((0,), (0,)), LOW)
    second_grad = mm(hidden_low[...], grads[0], ((0,), (0,)), LOW)
    for column in range(0, width, units):
        weights_out[0, width + column : width + column + units, :] = second_grad[
            :, column : column + units
        ]

    @pl.when(chunk == pl.num_programs(0) - 1)
    def _():
        y_out[...] = y_sum[...].astype(LOW)
        back_out[...] = back_sum[...].astype(LOW)


def run_expert(expert, rows, grads, weights):
    chunks, height, units = weights.shape
    count, width = rows.shape[1:]
    rows_in = pl.BlockSpec((1, count, width), lambda c: (expert, 0, 0))
    rows_out = pl.BlockSpec((count, width), lambda c: (0, 0))
    weight_spec = pl.BlockSpec((1, height, units), lambda c: (c, 0, 0))
    rows_shape = jax.ShapeDtypeStruct((count, width), LOW)
    return pl.pallas_call(
        expert_kernel,
        grid=(chunks,),
        in_specs=[rows_in, rows_in, weight_spec],
        out_specs=[rows_out, rows_out, weight_spec],
        out_shape=[rows_shape, rows_shape, jax.ShapeDtypeStruct(weights.shape, LOW)],
        scratch_shapes=[
            pltpu.VMEM((count, width), FULL),
            pltpu.VMEM((count, width), FULL),
            pltpu.VMEM((count, units), LOW),
            pltpu.VMEM((count, units), LOW),
        ],
        compiler_params=pltpu.CompilerParams(vmem_limit_bytes=VMEM_BYTES),
        cost_estimate=small_cost(
            flops=chunks * 12 * count * width * units,
            bytes_accessed=8 * count * width + 8 * chunks * width * units,
            transcendentals=2 * chunks * count * units,
        ),
        name="run_expert",
    )(rows, grads, weights)


def place_kernel(groups, hot, *refs):
    *parts, out = refs
    size = len(parts) // groups
    width = parts[0].shape[1]
    for group in range(groups):
        some = [part[...] for part in parts[group * size : (group + 1) * size]]
        values = jnp.concatenate(some, axis=0)
        out[0, :, group * width : (group + 1) * width] = mm(hot[0], values, ((1,), (0,)), LOW)


def place_rows(hot, groups, capacity):
    blocks, count, slots = hot.shape
    parts = sum(groups, [])
    width = parts[0].shape[1]
    wide = width * len(groups)
    return pl.pallas_call(
        partial(place_kernel, len(groups)),
        grid=(blocks,),
        in_specs=[pl.BlockSpec((1, count, slots), lambda b: (b, 0, 0))]
        + [pl.BlockSpec((capacity, width), lambda b: (b, 0))] * len(parts),
        out_specs=pl.BlockSpec((1, count, wide), lambda b: (b, 0, 0)),
        out_shape=jax.ShapeDtypeStruct((blocks, count, wide), LOW),
        compiler_params=pltpu.CompilerParams(vmem_limit_bytes=VMEM_BYTES),
        cost_estimate=small_cost(
            flops=2 * blocks * count * slots * wide,
            bytes_accessed=4 * blocks * count * wide,
            transcendentals=0,
        ),
        name="place_rows",
    )(hot, *parts)


def body(
    tokens,
    cotangent,
    seq_lens,
    routes,
    norm_gains,
    qkv_weight,
    out_weight,
    router_weight,
    rel_bias,
    expert_in,
    expert_out,
):
    tok_count, width = tokens.shape
    bucket_count = rel_bias.shape[0]
    shard_rows = qkv_weight.shape[0]
    experts_all = router_weight.shape[1]
    local_experts, _, units = expert_in.shape
    capacity = 2 * tok_count // experts_all
    places = lax.axis_size("fsdp") // 2
    place = lax.axis_index("fsdp") // 2
    peer = lax.axis_index("dp")
    peer_count = lax.axis_size("dp")
    core = ("dp", 1)
    dims = [("fsdp", 1)]
    mask = 2
    while mask < peer_count:
        dims.append(("dp", mask))
        mask *= 2

    spare = -(4 * width + experts_all + 2) % 128
    packed = jnp.concatenate(
        (
            qkv_weight,
            out_weight,
            router_weight,
            norm_gains.T,
            jnp.zeros((shard_rows, spare), LOW),
        ),
        axis=1,
    )
    dense, near = dense_gather(packed, places, place, dims, core)
    qkv_full = dense[:, : 3 * width]
    out_full = dense[:, 3 * width : 4 * width]
    router_full = dense[:, 4 * width : 4 * width + experts_all]
    gains_float = dense[:, 4 * width + experts_all : 4 * width + experts_all + 2].T.astype(FULL)

    groups = z_groups(places)
    weights = []
    for expert in range(local_experts):
        runs = [expert_out[expert][:, row : row + units] for row in range(0, width, units)]
        own = jnp.concatenate([expert_in[expert]] + runs)
        if expert > 0:
            (own,) = after((own,), (near,))
        weights.append(lax.all_gather(own, "fsdp", axis=0, axis_index_groups=groups))

    chosen = routes[:, 0]
    chosen_hot = chosen[:, None] == jnp.arange(experts_all, dtype=jnp.int32)[None, :]
    order = jnp.arange(tok_count, dtype=jnp.int32)
    earlier = (order[:, None] > order[None, :]).astype(LOW)
    rank_all = jnp.dot(earlier, chosen_hot.astype(LOW), preferred_element_type=FULL)
    rank_in = jnp.sum(jnp.where(chosen_hot, rank_all, 0.0), axis=1).astype(jnp.int32)
    slots_of = gather_blocks((chosen * capacity + rank_in)[None, :], dims)
    keys = sorted(slots_of)
    slots_near = jnp.stack([slots_of[key][0] for key in keys])
    local_slots = local_experts * capacity
    slot_ids = jnp.arange(local_slots, dtype=jnp.int32).reshape(local_experts, capacity)

    def hot_of(owner):
        wanted = owner * local_slots + slot_ids
        return (slots_near[:, None, None, :] == wanted[None, :, :, None]).astype(LOW)

    hot_own, hot_other = hot_of(peer), hot_of(peer ^ 1)
    segment = segment_ids(seq_lens[0], tok_count)
    bucket_hot = diagonal_hot(tok_count, bucket_count)
    base = jnp.einsum("rjb,bh->hrj", bucket_hot, rel_bias, precision=HIGH)

    inputs = tokens.astype(FULL)
    normed_one, inverse_one = rms_parts(inputs, gains_float[0])
    normed_low = normed_one.astype(LOW)
    projected = jnp.dot(normed_low, qkv_full, preferred_element_type=FULL).astype(LOW)
    attended, probs = attend_forward(projected, base, segment[:, None], segment[None, :])
    hidden_one = inputs + jnp.dot(attended, out_full, preferred_element_type=FULL)
    normed_two, inverse_two = rms_parts(hidden_one, gains_float[1])
    normed_two_low = normed_two.astype(LOW)
    router_soft = softmax_rows(jnp.dot(normed_two_low, router_full, preferred_element_type=FULL))
    gate_value = jnp.sum(jnp.where(chosen_hot, router_soft, 0.0), axis=1)
    upstream = cotangent.astype(FULL)
    grad_y = (gate_value[:, None] * upstream).astype(LOW)

    def pick(hot, blocks):
        return jnp.einsum("bjst,btd->jbsd", hot, blocks, preferred_element_type=FULL).astype(LOW)

    def to_rows(blocks):
        other = swap(pick(hot_other, blocks), core)
        both = jnp.stack((pick(hot_own, blocks), other), axis=1)
        return both.reshape(local_experts, -1, width)

    token_ids = jnp.concatenate((peer * local_slots + slot_ids, (peer ^ 1) * local_slots + slot_ids))
    hot_back = (slots_near[:, :, None] == token_ids.reshape(-1)[None, None, :]).astype(LOW)

    def from_rows(*groups):
        near_rows = len(keys) * capacity
        parts = [
            list(values) + [swap(value[near_rows:], core) for value in values] for values in groups
        ]
        return place_rows(hot_back, parts, capacity)

    blocks, brought = gather_halves(normed_two_low, dims)
    rows = to_rows(blocks)
    (grad_tied,) = after((grad_y,), brought[0])
    grad_blocks, _ = gather_halves(grad_tied, dims)
    grads = to_rows(grad_blocks)
    results = []
    for expert in range(local_experts):
        held = weights[expert]
        if expert > 0:
            (held,) = after((held,), (results[-1][0], hot_back))
        results.append(run_expert(expert, rows, grads, held))
    summed = [
        lax.psum_scatter(
            result[2], "fsdp", scatter_dimension=0, axis_index_groups=groups, tiled=False
        )
        for result in results
    ]
    returned = scatter_halves(
        from_rows(*[[result[which] for result in results] for which in (0, 1)]), keys, dims
    )
    token_y, grad_rows = returned[:, :width], returned[:, width:]

    mixed = (hidden_one + gate_value[:, None] * token_y).astype(LOW)
    grad_gate = jnp.sum(upstream * token_y, axis=1)
    grad_logits = router_soft * (
        jnp.where(chosen_hot, grad_gate[:, None], 0.0) - (gate_value * grad_gate)[:, None]
    )
    router_local = jnp.dot(normed_two_low.astype(FULL).T, grad_logits, precision=HIGH)
    grad_normed_two = grad_rows + jnp.dot(
        grad_logits, router_full.astype(FULL).T, precision=HIGH
    )
    grad_from_two, gain_grad_two = norm_back(
        hidden_one, inverse_two, gains_float[1], grad_normed_two
    )
    grad_hidden_one = upstream + grad_from_two
    grad_attn_low = grad_hidden_one.astype(LOW)
    out_local = jnp.einsum("td,te->de", attended, grad_attn_low, preferred_element_type=FULL)
    grad_attended = mm(grad_attn_low, out_full, ((1,), (1,)), LOW)
    names = ["z", dims[0]] + sorted(dims[1:], reverse=True) + [core]

    def split_rows(panel):
        shape = (places,) + (2,) * (len(names) - 1) + (shard_rows, panel.shape[1])
        parts, left, _ = halve([panel.reshape(shape)], [names], [core])
        return (parts[0], left[0])

    spare_out = -(experts_all + 2) % 128
    out_panel = jnp.concatenate(
        (
            out_local.astype(LOW),
            router_local.astype(LOW),
            gain_grad_two[:, None].astype(LOW),
            jnp.zeros((width, spare_out + 1), LOW),
        ),
        axis=1,
    )
    out_half, half_names = split_rows(out_panel)
    early = summed[:-1]
    (grad_attended,) = after((grad_attended,), early)
    *grad_parts, diagonals = attend_back(projected, grad_attended, probs, 0, HEADS // 2)
    grad_projected = jnp.concatenate(grad_parts, axis=1)
    qkv_local = mm(normed_low, grad_projected, ((0,), (0,)), LOW)
    qkv_half, _ = split_rows(qkv_local)
    half = 3 * width // 2
    grad_normed_one = mm(grad_projected, qkv_full, ((1,), (1,)))
    grad_from_one, gain_grad_one = norm_back(inputs, inverse_one, gains_float[0], grad_normed_one)
    tokens_grad = grad_hidden_one + grad_from_one
    bias_local = jnp.einsum("hrj,rjb->bh", diagonals, bucket_hot, precision=HIGH)
    gain_rows = width // 128
    small = jnp.concatenate((bias_local.reshape(-1, 128), gain_grad_one.reshape(-1, 128)))
    dense_sum, small = dense_scatter(
        [qkv_half[..., :half], qkv_half[..., half:], out_half],
        half_names,
        [dims, dims[::-1], dims[::-1]],
        groups,
        small,
    )
    summed[-1:] = after(summed[-1:], (dense_sum,))
    in_grad = jnp.stack([both[:width].astype(FULL) for both in summed])
    out_expert_grad = jnp.stack(
        [
            jnp.concatenate(
                [both[row : row + units].astype(FULL) for row in range(width, 2 * width, units)],
                axis=1,
            )
            for both in summed
        ]
    )
    qkv_grad, out_sum = dense_sum[:, : 3 * width], dense_sum[:, 3 * width :]
    bias_grad = small[:-gain_rows].reshape(bias_local.shape)
    device = lax.axis_index("fsdp") * peer_count + peer
    gain_one = lax.dynamic_slice_in_dim(
        small[-gain_rows:].reshape(-1), device * shard_rows, shard_rows
    )
    gains_grad = jnp.stack((gain_one, out_sum[:, width + experts_all]))
    router_grad = out_sum[:, width : width + experts_all]
    out_grad = out_sum[:, :width]
    return (
        mixed,
        tokens_grad,
        gains_grad,
        qkv_grad,
        out_grad,
        router_grad,
        bias_grad,
        in_grad,
        out_expert_grad,
    )


def solution(mesh):
    rows = P(("fsdp", "dp"), None)
    columns = P(None, ("fsdp", "dp"))
    experts = (P("dp", None, "fsdp"), P("dp", "fsdp", None))
    return jax.shard_map(
        body,
        mesh=mesh,
        in_specs=(rows, rows, rows, rows, columns, rows, rows, rows, P()) + experts,
        out_specs=(rows, rows, columns, rows, rows, rows, P()) + experts,
        check_vma=False,
    )
```
